256 devices in a mesh: row: 32 (over z, x), col: 8 (over y, core).
Axes of the slice: x: 4, y: 4, z: 8, core: 2. Of those that a mesh axis runs over, the one named last changes fastest.
Arguments:
- vectors: bfloat16 [256, 65536], P('col', 'row'), may hold values from -6 to 6
- hblocks: bfloat16 [1024, 12, 4096], P('row'), may hold values from -0.15625 to 0.15625
- counts: int32 [1024], P('row'), may hold values from 3 to 12, as said below
- sources: int32 [1024, 12], P('row'), may hold values from 0 to 95, as said below
- send_rows: int32 [2048], P('row'), may hold values from 0 to 31
Outputs:
- filtered: bfloat16 [256, 65536], P('col', 'row')
- gram_matrix: float32 [256, 256], P(None, 'col')
- projected: float32 [256, 256], P(None, 'col')
The draws below stay inside these ranges and needn't reach their ends.
Inputs may be any that keep to these rules, and one draw needn't show every extreme that they name: Blocks 0 to counts[i] - 1 of block row i are live; the rows of every device include one with 12 live blocks. `sources`: entry 0 of block row i is i's own index within its device. On every device each slot value 32 + s, s below 64, stands exactly once, at block 1 or 2 of some row. `send_rows`: entries p * 64 + q * 2 + c name block rows of device p within it.
All inputs are finite; a program needn't handle non-finite values.
Results may differ from the reference program's by a relative error of at most 0.017.
Values may be sent and summed in bfloat16 or wider, within the bound.
No kernel may reach another device: no remote copies, remote signals or barrier semaphores. Data moves between devices by JAX's collectives and lax.ppermute only.
A program may use at most 128 MiB of HBM per device.

```python
import jax
import jax.numpy as jnp
from jax import lax

B = 64
M = 256
K = 12
C = 2
RB = 32
NB = 1024
SLOTS = 64
N = 65536
N_ROW = 32


def draw_counts(key, part):
    values = jax.random.randint(key, (NB,), 3, K + 1, dtype=jnp.int32)
    chosen_rows = jax.random.randint(jax.random.fold_in(key, 5), (NB // RB,), 0, RB, dtype=jnp.int32)
    return values.at[jnp.arange(NB // RB, dtype=jnp.int32) * RB + chosen_rows].set(K)


def draw_sources(key, part):
    devices = NB // RB

    def per_device(device):
        device_key = jax.random.fold_in(key, device)
        entries = jax.random.randint(jax.random.fold_in(device_key, 1), (RB, K), 0, RB, dtype=jnp.int32)
        entries = entries.at[:, 0].set(jnp.arange(RB, dtype=jnp.int32))
        shuffle = jax.random.permutation(jax.random.fold_in(device_key, 2), RB)
        positions = jnp.arange(SLOTS, dtype=jnp.int32)
        return entries.at[shuffle[positions % RB], 1 + positions // RB].set(RB + positions)
    return jax.vmap(per_device)(jnp.arange(devices, dtype=jnp.int32)).reshape(NB, K)


def touch_ends(values, own_key, low, largest):
    longest = values.shape.index(max(values.shape))
    spots = []
    for shift in (0, 1):
        where = [jax.random.randint(jax.random.fold_in(own_key, axis), (), 0, length) for axis, length in enumerate(values.shape)]
        where[longest] = (where[longest] + shift) % values.shape[longest]
        spots.append(tuple(where))
    return values.at[spots[0]].set(low).at[spots[1]].set(largest)


def block_scale(stream_key, dims, split, least, largest):
    gain = 1.0
    for position, parts in split:
        heights = jax.random.uniform(jax.random.fold_in(jax.random.fold_in(stream_key, 6), position), (parts,), jnp.float32, least / len(split), largest / len(split))
        gain = gain * jnp.repeat(jnp.exp(heights), dims[position] // parts).reshape((-1,) + (1,) * (len(dims) - 1 - position))
    return gain


def normal_values(rng, shape, width, bound, pieces=(), kind=jnp.bfloat16):
    gain = block_scale(rng, shape, pieces, -0.22, 0.18) if pieces else 1.0
    values = jax.random.normal(rng, shape, jnp.float32) * width * gain
    return jnp.minimum(jnp.maximum(values, -bound), bound).astype(kind)


def setup_inputs(seed: int = 0) -> dict:
    keys = jax.random.split(jax.random.key(seed), 6)
    vectors = normal_values(keys[0], (M, N), 1.0, 6.0, ((0, 8), (1, 32)))
    hblocks = normal_values(keys[1], (NB, K, B * B), (2 * K * B) ** -0.5, 0.15625, ((0, 32),))
    counts = draw_counts(jax.random.fold_in(keys[5], 71), 0)
    sources = draw_sources(jax.random.fold_in(keys[5], 71), 0)
    send_rows = touch_ends(jax.random.randint(keys[4], (N_ROW * SLOTS,), 0, RB), jax.random.fold_in(keys[4], 1), 0, RB - 1).astype(jnp.int32)
    return dict(vectors=vectors, hblocks=hblocks, counts=counts, sources=sources, send_rows=send_rows)


center_value = 0.25
half_width = 1.5


def column_blocks(sources, send_rows):
    row_index = jnp.arange(NB, dtype=jnp.int32)[:, None]
    owner_row = row_index // RB
    slot_index = jnp.maximum(sources - RB, 0)
    peer_index = slot_index // C
    within_peer = slot_index % C
    remote = peer_index * RB + send_rows[(peer_index * SLOTS + owner_row * C + within_peer).astype(jnp.int32)]
    return jnp.where(sources < RB, owner_row * RB + sources, remote).astype(jnp.int32)


def apply_operator(block_vectors, masked, gcol):
    def accumulate(group, accum):
        offset = (group * RB).astype(jnp.int32)
        group_blocks = lax.dynamic_slice_in_dim(masked, offset, RB, 0).astype(jnp.float32)
        group_columns = lax.dynamic_slice_in_dim(gcol, offset, RB, 0)
        group_vectors = lax.dynamic_slice_in_dim(block_vectors, offset, RB, 0).astype(jnp.float32)
        picked = block_vectors[group_columns].astype(jnp.float32)
        upper_part = jnp.einsum("ikmb,ikab->ima", picked, group_blocks, precision=lax.Precision.HIGHEST)
        mirror = jnp.einsum("ima,ikab->ikmb", group_vectors, group_blocks, precision=lax.Precision.HIGHEST)
        current = lax.dynamic_slice_in_dim(accum, offset, RB, 0)
        accum = lax.dynamic_update_slice_in_dim(accum, current + upper_part, offset, 0)
        return accum.at[group_columns.reshape(-1)].add(mirror.reshape(RB * K, M, B))
    return lax.fori_loop(0, NB // RB, accumulate, jnp.zeros((NB, M, B), jnp.float32))


def reference(vectors, hblocks, counts, sources, send_rows):
    gcol = column_blocks(sources, send_rows)
    live_mask = jnp.arange(K, dtype=jnp.int32)[None, :] < counts[:, None]
    masked = jnp.where(live_mask[:, :, None], hblocks, jnp.zeros((), hblocks.dtype)).reshape(NB, K, B, B)
    start_blocks = vectors.reshape(M, NB, B).transpose(1, 0, 2)
    start_float = start_blocks.astype(jnp.float32)
    first_image = apply_operator(start_blocks, masked, gcol)
    first_step = ((first_image - center_value * start_float) / half_width).astype(jnp.bfloat16)
    second_image = apply_operator(first_step, masked, gcol)
    second_step = (2.0 * (second_image - center_value * first_step.astype(jnp.float32)) / half_width - start_float).astype(jnp.bfloat16)
    image_blocks = apply_operator(second_step, masked, gcol).astype(jnp.bfloat16)
    filtered = second_step.transpose(1, 0, 2).reshape(M, NB * B)
    image_rows = image_blocks.transpose(1, 0, 2).reshape(M, NB * B)
    gram_matrix = jnp.dot(filtered, filtered.T, preferred_element_type=jnp.float32)
    projected = jnp.dot(filtered, image_rows.T, preferred_element_type=jnp.float32)
    return (filtered, gram_matrix, projected)
```

```python
import jax
import jax.numpy as jnp
from jax import lax
from jax.experimental import pallas as pl
from jax.experimental.pallas import tpu as pltpu
from jax.sharding import Mesh, PartitionSpec as P

B = 64
K = 12
RB = 32
MC = 32
PEERS = 32
NZ, NX, NY, NC = 8, 4, 4, 2
STEP = 8
LOCAL = ((0, 3), (4, 5), (6, 7), (8, 9), (10, 11))
LW = 128 * len(LOCAL)
center_value = 0.25
half_width = 1.5
bf16 = jnp.bfloat16
f32 = jnp.float32
VMEM_LIMIT = 40 * 1024 * 1024

NN = (((1,), (0,)), ((), ()))
NT = (((1,), (1,)), ((), ()))


def low_half(rows=MC):
    return lax.broadcasted_iota(jnp.int32, (rows, 128), 1) < B


def dot(a, b, dims):
    return lax.dot_general(a, b, dims, preferred_element_type=f32)


def store_pair(even_odd_ref, first, second, low):
    even_odd_ref[pl.ds(0, 32, stride=2), :] = jnp.where(low, first, pltpu.roll(second, B, 1))
    even_odd_ref[pl.ds(1, 32, stride=2), :] = jnp.where(low, pltpu.roll(first, B, 1), second)


def duplicate(tile, low):
    turned = pltpu.roll(tile, B, 1)
    return jnp.where(low, tile, turned), jnp.where(low, turned, tile)


def emit_picks(msg_ref, dup_ref, send_ref, low):
    for q in range(PEERS):
        msg_ref[q, 0:MC, :] = jnp.where(
            low, dup_ref[send_ref[2 * q]], dup_ref[send_ref[2 * q + 1]]
        ).astype(bf16)


def emit_mirror(msg_ref, prod_ref, inv_ref, low):
    for q in range(PEERS):
        msg_ref[q, MC : 2 * MC, :] = jnp.where(
            low, prod_ref[inv_ref[2 * q]], prod_ref[inv_ref[2 * q + 1]]
        ).astype(bf16)


def invert_slots(inv_ref, src_ref):
    for i in range(RB):
        for k in (1, 2):
            inv_ref[src_ref[i, k] - RB] = 2 * i + k - 1


def first_message_kernel(src_ref, send_ref, v_ref, hb_ref, msg_ref, wd_ref, rows_ref, pair_ref, dup_ref, prod_ref, inv_ref):
    step = pl.program_id(0)
    low = low_half()

    @pl.when(step == 0)
    def _():
        for t in range(RB // 2):
            tile = v_ref[:, 128 * t : 128 * (t + 1)].astype(f32)
            dup_ref[2 * t], dup_ref[2 * t + 1] = duplicate(tile, low)
        invert_slots(inv_ref, src_ref)
        emit_picks(msg_ref, dup_ref, send_ref, low)

    for il in range(STEP):
        for j in range(32):
            rows_ref[il, 8 * j : 8 * (j + 1), :] = hb_ref[il, 0:8, 128 * j : 128 * (j + 1)].astype(f32)
        for k in (1, 2):
            block = rows_ref[il, pl.ds(k, 32, stride=8), :]
            store_pair(pair_ref.at[2 * il + k - 1], block, block, low)
        wd_ref[il, :, 0:128] = pair_ref[2 * il].astype(bf16)
        wd_ref[il, :, 128:256] = pair_ref[2 * il + 1].astype(bf16)
    for il in range(STEP):
        i = step * STEP + il
        prod = dot(dup_ref[i][:, 0:B].astype(bf16), wd_ref[il], NN)
        prod_ref[2 * i] = prod[:, 0:128]
        prod_ref[2 * i + 1] = prod[:, 128:256]

    @pl.when(step == RB // STEP - 1)
    def _():
        emit_mirror(msg_ref, prod_ref, inv_ref, low)


def local_product(src_ref, v_ref, um_ref, y_ref, dup_ref, dupb_ref, lhs_ref, mir_ref, acc_ref):
    low = low_half()
    for t in range(RB // 2):
        tile = v_ref[:, 128 * t : 128 * (t + 1)].astype(f32)
        one, two = duplicate(tile, low)
        dup_ref[2 * t], dup_ref[2 * t + 1] = one, two
        dupb_ref[2 * t], dupb_ref[2 * t + 1] = one.astype(bf16), two.astype(bf16)

    def gather(i, _):
        for t, (k0, k1) in enumerate(LOCAL):
            j0 = i if k0 == 0 else jnp.minimum(src_ref[i, k0], RB - 1)
            j1 = jnp.minimum(src_ref[i, k1], RB - 1)
            lhs_ref[i, :, 128 * t : 128 * (t + 1)] = jnp.where(low, dup_ref[j0], dup_ref[j1]).astype(bf16)
        return 0

    lax.fori_loop(0, RB, gather, 0, unroll=4)
    for i in range(RB):
        mir_ref[i] = dot(dupb_ref[i][:, 0:B], um_ref[i], NN)
    for i in range(RB):
        acc_ref[i, :, 0:B] = dot(lhs_ref[i], um_ref[i], NT)
        acc_ref[i, :, B:128] = jnp.zeros((MC, B), f32)

    def scatter(i, _):
        for t, (k0, k1) in enumerate(LOCAL):
            j0 = i if k0 == 0 else jnp.minimum(src_ref[i, k0], RB - 1)
            j1 = jnp.minimum(src_ref[i, k1], RB - 1)
            part = mir_ref[i, :, 128 * t : 128 * (t + 1)]
            acc_ref[j0] += jnp.where(low, part, 0.0)
            acc_ref[j1] += jnp.where(low, 0.0, part)
        return 0

    lax.fori_loop(0, RB, scatter, 0, unroll=4)
    for t in range(RB // 2):
        one, two = acc_ref[2 * t], acc_ref[2 * t + 1]
        y_ref[:, 128 * t : 128 * (t + 1)] = jnp.where(
            low, one + pltpu.roll(one, B, 1), two + pltpu.roll(two, B, 1)
        )


def first_local_kernel(src_ref, counts_ref, v_ref, hb_ref, um_ref, y_ref, rows_ref, pair_ref, dup_ref, dupb_ref, lhs_ref, mir_ref, acc_ref):
    step = pl.program_id(0)
    low = low_half()
    for il in range(STEP):
        i = step * STEP + il
        count = counts_ref[i]
        for j in range(32):
            rows_ref[il, 16 * j : 16 * j + K, :] = hb_ref[il, :, 128 * j : 128 * (j + 1)].astype(f32)
        for t, (k0, k1) in enumerate(LOCAL):
            one = rows_ref[il, pl.ds(k0, 32, stride=16), :]
            two = rows_ref[il, pl.ds(k1, 32, stride=16), :]
            if k0 >= 3:
                one = jnp.where(k0 < count, one, 0.0)
            two = jnp.where(k1 < count, two, 0.0)
            pair = pair_ref.at[il * len(LOCAL) + t]
            store_pair(pair, one, two, low)
            um_ref[i, :, 128 * t : 128 * (t + 1)] = pair[...].astype(bf16)

    @pl.when(step == RB // STEP - 1)
    def _():
        local_product(src_ref, v_ref, um_ref, y_ref, dup_ref, dupb_ref, lhs_ref, mir_ref, acc_ref)


def remote_sum(src_ref, send_ref, recv_ref, wd_ref, lhs_ref, acc_ref):
    low = low_half()
    lane = lax.broadcasted_iota(jnp.int32, (MC, 128), 1) // B

    def gather(i, _):
        for k in (1, 2):
            s = src_ref[i, k] - RB
            tile = recv_ref[s // 2, 0:MC, :].astype(f32)
            lhs_ref[i, :, 128 * (k - 1) : 128 * k] = jnp.where(lane == s % 2, tile, 0.0).astype(bf16)
        return 0

    lax.fori_loop(0, RB, gather, 0, unroll=4)
    for i in range(RB):
        acc_ref[i, :, 0:B] = dot(lhs_ref[i], wd_ref[i], NT)
        acc_ref[i, :, B:128] = jnp.zeros((MC, B), f32)

    def scatter(q, _):
        tile = recv_ref[q, MC : 2 * MC, :].astype(f32)
        acc_ref[send_ref[2 * q]] += jnp.where(low, tile, 0.0)
        acc_ref[send_ref[2 * q + 1]] += jnp.where(low, 0.0, tile)
        return 0

    lax.fori_loop(0, PEERS, scatter, 0, unroll=4)


def folded(acc_ref, t, low):
    one, two = acc_ref[2 * t], acc_ref[2 * t + 1]
    return jnp.where(low, one + pltpu.roll(one, B, 1), two + pltpu.roll(two, B, 1))


def step_kernel(second, src_ref, send_ref, recv_ref, y_ref, v_ref, prev_ref, wd_ref, out_ref, msg_ref, lhs_ref, acc_ref, dup_ref, prod_ref, inv_ref):
    low = low_half()
    invert_slots(inv_ref, src_ref)
    remote_sum(src_ref, send_ref, recv_ref, wd_ref, lhs_ref, acc_ref)
    for t in range(RB // 2):
        lanes = slice(128 * t, 128 * (t + 1))
        image = folded(acc_ref, t, low) + y_ref[:, lanes]
        if second:
            tile = 2.0 * (image - center_value * prev_ref[:, lanes].astype(f32)) / half_width - v_ref[:, lanes].astype(f32)
        else:
            tile = (image - center_value * v_ref[:, lanes].astype(f32)) / half_width
        tile = tile.astype(bf16)
        out_ref[:, lanes] = tile
        dup_ref[2 * t], dup_ref[2 * t + 1] = duplicate(tile.astype(f32), low)
    emit_picks(msg_ref, dup_ref, send_ref, low)
    for i in range(RB):
        prod = dot(dup_ref[i][:, 0:B].astype(bf16), wd_ref[i], NN)
        prod_ref[2 * i] = prod[:, 0:128]
        prod_ref[2 * i + 1] = prod[:, 128:256]
    emit_mirror(msg_ref, prod_ref, inv_ref, low)


def image_kernel(src_ref, send_ref, recv_ref, y_ref, f_ref, all_ref, wd_ref, out_ref, lhs_ref, acc_ref, stack_ref):
    low = low_half()
    remote_sum(src_ref, send_ref, recv_ref, wd_ref, lhs_ref, acc_ref)
    stack_ref[0:MC, :] = f_ref[...]
    for t in range(RB // 2):
        lanes = slice(128 * t, 128 * (t + 1))
        stack_ref[MC : 2 * MC, lanes] = (folded(acc_ref, t, low) + y_ref[:, lanes]).astype(bf16)
    part = dot(stack_ref[...], all_ref[...], NT).astype(bf16)
    for z in range(NZ):
        out_ref[z] = part


def sum_z_kernel(in_ref, out_ref):
    total = in_ref[0].astype(f32)
    for z in range(1, NZ):
        total = total + in_ref[z].astype(f32)
    total = total.astype(bf16)
    for x in range(NX):
        out_ref[x] = total


def sum_x_kernel(in_ref, gram_ref, proj_ref):
    total = in_ref[0].astype(f32)
    for x in range(1, NX):
        total = total + in_ref[x].astype(f32)
    gram_ref[...] = total[0:MC, :].T
    proj_ref[...] = total[MC : 2 * MC, :].T


SMEM = pl.BlockSpec(memory_space=pltpu.SMEM)
VM = pl.BlockSpec(memory_space=pltpu.VMEM)
params = pltpu.CompilerParams(vmem_limit_bytes=VMEM_LIMIT)
shape = jax.ShapeDtypeStruct


def on_device(vectors, hblocks, counts, sources, send_rows):
    cols, width = vectors.shape
    row_axes, rows = ("z", "x"), hblocks.shape[0]
    msg_shape = shape((PEERS, 2 * MC, 128), bf16)
    wd_shape = shape((rows, B, 256), bf16)
    dup = pltpu.VMEM((rows, MC, 128), f32)
    dupb = pltpu.VMEM((rows, MC, 128), bf16)
    acc = pltpu.VMEM((rows, MC, 128), f32)
    prod = pltpu.VMEM((2 * rows, MC, 128), f32)
    inv = pltpu.SMEM((2 * PEERS,), jnp.int32)
    lhs = pltpu.VMEM((rows, MC, LW), bf16)
    lhs_remote = pltpu.VMEM((rows, MC, 256), bf16)
    mir = pltpu.VMEM((rows, MC, LW), f32)

    def whole(shape_):
        return pl.BlockSpec(shape_, lambda g: (0,) * len(shape_))

    grid_rows = pl.BlockSpec((STEP, K, B * B), lambda g: (g, 0, 0))
    message, wd = pl.pallas_call(
        first_message_kernel,
        grid=(rows // STEP,),
        out_shape=(msg_shape, wd_shape),
        in_specs=[SMEM, SMEM, whole((cols, width)), grid_rows],
        out_specs=(whole(msg_shape.shape), pl.BlockSpec((STEP, B, 256), lambda g: (g, 0, 0))),
        scratch_shapes=[
            pltpu.VMEM((STEP, 256, 128), f32),
            pltpu.VMEM((2 * STEP, B, 128), f32),
            dup,
            prod,
            inv,
        ],
        compiler_params=params,
        name="first_message",
    )(sources, send_rows, vectors, hblocks)

    def exchange(message):
        return lax.all_to_all(message, row_axes, split_axis=0, concat_axis=0, tiled=True)

    received = exchange(message)
    local_scratch = [dup, dupb, lhs, mir, acc]
    um, local = pl.pallas_call(
        first_local_kernel,
        grid=(rows // STEP,),
        out_shape=(shape((rows, B, LW), bf16), shape((cols, width), f32)),
        in_specs=[SMEM, SMEM, whole((cols, width)), grid_rows],
        out_specs=(whole((rows, B, LW)), whole((cols, width))),
        scratch_shapes=[
            pltpu.VMEM((STEP, 512, 128), f32),
            pltpu.VMEM((STEP * len(LOCAL), B, 128), f32),
        ]
        + local_scratch,
        compiler_params=params,
        name="first_local",
    )(sources, counts, vectors, hblocks)

    def local_part(block):
        return pl.pallas_call(
            local_product,
            out_shape=shape((cols, width), f32),
            in_specs=[SMEM, VM, VM],
            out_specs=VM,
            scratch_shapes=local_scratch,
            compiler_params=params,
            name="local_product",
        )(sources, block, um)

    def next_step(second, received, local, previous):
        return pl.pallas_call(
            lambda *refs: step_kernel(second, *refs),
            out_shape=(shape((cols, width), bf16), msg_shape),
            in_specs=[SMEM, SMEM] + [VM] * 5,
            out_specs=(VM, VM),
            scratch_shapes=[lhs_remote, acc, dup, prod, inv],
            compiler_params=params,
            name="second_step" if second else "first_step",
        )(sources, send_rows, received, local, vectors, previous, wd)

    first, message = next_step(False, received, local, vectors)
    received = exchange(message)
    local = local_part(first)
    filtered, message = next_step(True, received, local, first)
    received = exchange(message)
    local = local_part(filtered)
    both = lax.all_gather(filtered, "c", axis=0, tiled=True)
    everyone = lax.all_gather(both, "y", axis=0, tiled=True)
    part = pl.pallas_call(
        image_kernel,
        out_shape=shape((NZ, 2 * MC, NY * NC * MC), bf16),
        in_specs=[SMEM, SMEM] + [VM] * 5,
        out_specs=VM,
        scratch_shapes=[lhs_remote, acc, pltpu.VMEM((2 * MC, width), bf16)],
        compiler_params=params,
        name="image",
    )(sources, send_rows, received, local, filtered, everyone, wd)
    part = lax.all_to_all(part, "z", split_axis=0, concat_axis=0, tiled=True)
    part = pl.pallas_call(
        sum_z_kernel,
        out_shape=shape((NX,) + part.shape[1:], bf16),
        compiler_params=params,
        name="sum_z",
    )(part)
    part = lax.all_to_all(part, "x", split_axis=0, concat_axis=0, tiled=True)
    gram, projected = pl.pallas_call(
        sum_x_kernel,
        out_shape=(shape((NY * NC * MC, MC), f32),) * 2,
        compiler_params=params,
        name="sum_x",
    )(part)
    return filtered, gram, projected


def solution(mesh):
    axes = Mesh(mesh.devices.reshape(NZ, NX, NY, NC), ("z", "x", "y", "c"))
    row, col = ("z", "x"), ("y", "c")
    return jax.shard_map(
        on_device,
        mesh=axes,
        in_specs=(P(col, row), P(row, None, None), P(row), P(row, None), P(row)),
        out_specs=(P(col, row), P(None, col), P(None, col)),
        check_vma=False,
    )
```

```python
import jax
import jax.numpy as jnp
from jax import lax
from jax.experimental import pallas as pl
from jax.experimental.pallas import tpu as pltpu
from jax.sharding import Mesh, PartitionSpec as P

B = 64
K = 12
RB = 32
MC = 32
PEERS = 32
NZ, NX, NY, NC = 8, 4, 4, 2
SEND, COUNT = 12, 13
LOCAL = ((0, 3), (4, 5), (6, 7), (8, 9), (10, 11))
LW = 128 * len(LOCAL)
center_value = 0.25
half_width = 1.5
bf16 = jnp.bfloat16
f32 = jnp.float32
MIB = 1024 * 1024

NN = (((1,), (0,)), ((), ()))
NT = (((1,), (1,)), ((), ()))


def low_half(rows=MC):
    return lax.broadcasted_iota(jnp.int32, (rows, 128), 1) < B


def dot(a, b, dims):
    return lax.dot_general(a, b, dims, preferred_element_type=f32)


def store_pair(even_odd_ref, first, second, low):
    even_odd_ref[pl.ds(0, 32, stride=2), :] = jnp.where(low, first, pltpu.roll(second, B, 1))
    even_odd_ref[pl.ds(1, 32, stride=2), :] = jnp.where(low, pltpu.roll(first, B, 1), second)


def duplicate(tile, low):
    turned = pltpu.roll(tile, B, 1)
    return jnp.where(low, tile, turned), jnp.where(low, turned, tile)


def emit_picks(msg_ref, dup_ref, idx_ref, low):
    for q in range(PEERS):
        msg_ref[q, 0:MC, :] = jnp.where(
            low, dup_ref[idx_ref[SEND, 2 * q]], dup_ref[idx_ref[SEND, 2 * q + 1]]
        ).astype(bf16)


def emit_mirror(msg_ref, prod_ref, inv_ref, low):
    for q in range(PEERS):
        msg_ref[q, MC : 2 * MC, :] = jnp.where(
            low, prod_ref[inv_ref[2 * q]], prod_ref[inv_ref[2 * q + 1]]
        ).astype(bf16)


def invert_slots(inv_ref, idx_ref):
    for i in range(RB):
        for k in (1, 2):
            inv_ref[idx_ref[k, i] - RB] = 2 * i + k - 1


def unpack_rows(rows_ref, hb_ref):
    for j in range(32):
        rows_ref[32 * j : 32 * (j + 1), :] = hb_ref[0, :, 128 * j : 128 * (j + 1)].astype(f32)


def first_message_kernel(src_ref, send_ref, srcv_ref, sendv_ref, countv_ref, v_ref, hb_ref, idx_ref, msg_ref, wd_ref, rows_ref, pair_ref, dup_ref, prod_ref, inv_ref):
    step = pl.program_id(0)
    low = low_half()

    @pl.when(step == 0)
    def _():
        idx_ref[...] = jnp.zeros(idx_ref.shape, jnp.int32)
        idx_ref[0:K, 0:RB] = srcv_ref[...]
        idx_ref[SEND : SEND + 1, 0 : 2 * PEERS] = sendv_ref[...]
        idx_ref[COUNT : COUNT + 1, 0:RB] = countv_ref[...]
        for t in range(RB // 2):
            tile = v_ref[:, 128 * t : 128 * (t + 1)].astype(f32)
            dup_ref[2 * t], dup_ref[2 * t + 1] = duplicate(tile, low)
        for i in range(RB):
            for k in (1, 2):
                inv_ref[src_ref[k, i] - RB] = 2 * i + k - 1
        for q in range(PEERS):
            msg_ref[q, 0:MC, :] = jnp.where(
                low, dup_ref[send_ref[2 * q]], dup_ref[send_ref[2 * q + 1]]
            ).astype(bf16)

    unpack_rows(rows_ref, hb_ref)
    for i in range(RB):
        block = rows_ref[pl.ds(i, 32, stride=32), :]
        store_pair(pair_ref.at[i], block, block, low)

    @pl.when(step == 0)
    def _():
        for i in range(RB):
            wd_ref[i, :, 0:128] = pair_ref[i].astype(bf16)

    @pl.when(step == 1)
    def _():
        for i in range(RB):
            wd_ref[i, :, 128:256] = pair_ref[i].astype(bf16)
        mirror_products(dup_ref, wd_ref, prod_ref)
        emit_mirror(msg_ref, prod_ref, inv_ref, low)


def mirror_products(dup_ref, wd_ref, prod_ref):
    for i in range(RB):
        prod = dot(dup_ref[i][:, 0:B].astype(bf16), wd_ref[i], NN)
        prod_ref[2 * i] = prod[:, 0:128]
        prod_ref[2 * i + 1] = prod[:, 128:256]


def local_product(idx_ref, v_ref, um_ref, y_ref, dup_ref, dupb_ref, lhs_ref, mir_ref, acc_ref):
    low = low_half()
    for t in range(RB // 2):
        tile = v_ref[:, 128 * t : 128 * (t + 1)].astype(f32)
        one, two = duplicate(tile, low)
        dup_ref[2 * t], dup_ref[2 * t + 1] = one, two
        dupb_ref[2 * t], dupb_ref[2 * t + 1] = one.astype(bf16), two.astype(bf16)

    def gather(i, _):
        for t, (k0, k1) in enumerate(LOCAL):
            j0 = i if k0 == 0 else jnp.minimum(idx_ref[k0, i], RB - 1)
            j1 = jnp.minimum(idx_ref[k1, i], RB - 1)
            lhs_ref[i, :, 128 * t : 128 * (t + 1)] = jnp.where(low, dup_ref[j0], dup_ref[j1]).astype(bf16)
        return 0

    lax.fori_loop(0, RB, gather, 0, unroll=4)
    for i in range(RB):
        mir_ref[i] = dot(dupb_ref[i][:, 0:B], um_ref[i], NN)
    for i in range(RB):
        acc_ref[i, :, 0:B] = dot(lhs_ref[i], um_ref[i], NT)
        acc_ref[i, :, B:128] = jnp.zeros((MC, B), f32)

    def scatter(i, _):
        for t, (k0, k1) in enumerate(LOCAL):
            j0 = i if k0 == 0 else jnp.minimum(idx_ref[k0, i], RB - 1)
            j1 = jnp.minimum(idx_ref[k1, i], RB - 1)
            part = mir_ref[i, :, 128 * t : 128 * (t + 1)]
            acc_ref[j0] += jnp.where(low, part, 0.0)
            acc_ref[j1] += jnp.where(low, 0.0, part)
        return 0

    lax.fori_loop(0, RB, scatter, 0, unroll=4)
    for t in range(RB // 2):
        one, two = acc_ref[2 * t], acc_ref[2 * t + 1]
        y_ref[:, 128 * t : 128 * (t + 1)] = jnp.where(
            low, one + pltpu.roll(one, B, 1), two + pltpu.roll(two, B, 1)
        )


def first_local_kernel(idx_ref, v_ref, one_ref, two_ref, um_ref, y_ref, rows1_ref, rows2_ref, pair_ref, dup_ref, dupb_ref, lhs_ref, mir_ref, acc_ref):
    step = pl.program_id(0)
    low = low_half()
    unpack_rows(rows1_ref, one_ref)
    unpack_rows(rows2_ref, two_ref)
    k0, k1 = jnp.where(step == 0, 0, 2 * step + 2), 2 * step + 3
    lanes = pl.ds(pl.multiple_of(step * 128, 128), 128)
    for i in range(RB):
        count = idx_ref[COUNT, i]
        one = jnp.where(k0 < count, rows1_ref[pl.ds(i, 32, stride=32), :], 0.0)
        two = jnp.where(k1 < count, rows2_ref[pl.ds(i, 32, stride=32), :], 0.0)
        store_pair(pair_ref.at[i], one, two, low)
        um_ref[i, :, lanes] = pair_ref[i].astype(bf16)

    @pl.when(step == len(LOCAL) - 1)
    def _():
        local_product(idx_ref, v_ref, um_ref, y_ref, dup_ref, dupb_ref, lhs_ref, mir_ref, acc_ref)


def remote_sum(idx_ref, recv_ref, wd_ref, lhs_ref, acc_ref):
    low = low_half()
    lane = lax.broadcasted_iota(jnp.int32, (MC, 128), 1) // B

    def gather(i, _):
        for k in (1, 2):
            s = idx_ref[k, i] - RB
            tile = recv_ref[s // 2, 0:MC, :].astype(f32)
            lhs_ref[i, :, 128 * (k - 1) : 128 * k] = jnp.where(lane == s % 2, tile, 0.0).astype(bf16)
        return 0

    lax.fori_loop(0, RB, gather, 0, unroll=4)
    for i in range(RB):
        acc_ref[i, :, 0:B] = dot(lhs_ref[i], wd_ref[i], NT)
        acc_ref[i, :, B:128] = jnp.zeros((MC, B), f32)

    def scatter(q, _):
        tile = recv_ref[q, MC : 2 * MC, :].astype(f32)
        acc_ref[idx_ref[SEND, 2 * q]] += jnp.where(low, tile, 0.0)
        acc_ref[idx_ref[SEND, 2 * q + 1]] += jnp.where(low, 0.0, tile)
        return 0

    lax.fori_loop(0, PEERS, scatter, 0, unroll=4)


def folded(acc_ref, t, low):
    one, two = acc_ref[2 * t], acc_ref[2 * t + 1]
    return jnp.where(low, one + pltpu.roll(one, B, 1), two + pltpu.roll(two, B, 1))


def step_kernel(second, idx_ref, recv_ref, y_ref, v_ref, prev_ref, wd_ref, out_ref, msg_ref, lhs_ref, acc_ref, dup_ref, prod_ref, inv_ref):
    low = low_half()
    invert_slots(inv_ref, idx_ref)
    remote_sum(idx_ref, recv_ref, wd_ref, lhs_ref, acc_ref)
    for t in range(RB // 2):
        lanes = slice(128 * t, 128 * (t + 1))
        image = folded(acc_ref, t, low) + y_ref[:, lanes]
        if second:
            tile = 2.0 * (image - center_value * prev_ref[:, lanes].astype(f32)) / half_width - v_ref[:, lanes].astype(f32)
        else:
            tile = (image - center_value * v_ref[:, lanes].astype(f32)) / half_width
        tile = tile.astype(bf16)
        out_ref[:, lanes] = tile
        dup_ref[2 * t], dup_ref[2 * t + 1] = duplicate(tile.astype(f32), low)
    emit_picks(msg_ref, dup_ref, idx_ref, low)
    mirror_products(dup_ref, wd_ref, prod_ref)
    emit_mirror(msg_ref, prod_ref, inv_ref, low)


def image_kernel(idx_ref, recv_ref, y_ref, wd_ref, *refs):
    own, other = refs[0:NY], refs[NY : 2 * NY]
    out_ref, lhs_ref, acc_ref, stack_ref, all_ref = refs[2 * NY :]
    low = low_half()
    y, c = lax.axis_index("y"), lax.axis_index("c")
    for d in range(NY):
        from_y = lax.rem(y + NY - d, NY) * NC
        all_ref[pl.ds(pl.multiple_of((from_y + c) * MC, MC), MC), :] = own[d][...]
        all_ref[pl.ds(pl.multiple_of((from_y + 1 - c) * MC, MC), MC), :] = other[d][...]
    remote_sum(idx_ref, recv_ref, wd_ref, lhs_ref, acc_ref)
    stack_ref[0:MC, :] = own[0][...]
    for t in range(RB // 2):
        lanes = slice(128 * t, 128 * (t + 1))
        stack_ref[MC : 2 * MC, lanes] = (folded(acc_ref, t, low) + y_ref[:, lanes]).astype(bf16)
    part = dot(stack_ref[...], all_ref[...], NT).astype(bf16)
    for z in range(NZ):
        out_ref[z] = part


def sum_z_kernel(in_ref, out_ref):
    total = in_ref[0].astype(f32)
    for z in range(1, NZ):
        total = total + in_ref[z].astype(f32)
    total = total.astype(bf16)
    for x in range(NX):
        out_ref[x] = total


def sum_x_kernel(in_ref, gram_ref, proj_ref):
    total = in_ref[0].astype(f32)
    for x in range(1, NX):
        total = total + in_ref[x].astype(f32)
    gram_ref[...] = total[0:MC, :]
    proj_ref[...] = total[MC : 2 * MC, :]


SMEM = pl.BlockSpec(memory_space=pltpu.SMEM)
VM = pl.BlockSpec(memory_space=pltpu.VMEM)
shape = jax.ShapeDtypeStruct


def limit(mib):
    return pltpu.CompilerParams(vmem_limit_bytes=mib * MIB)


def on_device(vectors, hblocks, counts, sources, send_rows):
    cols, width = vectors.shape
    row_axes, rows = ("z", "x"), hblocks.shape[0]
    msg_shape = shape((PEERS, 2 * MC, 128), bf16)
    wd_shape = shape((rows, B, 256), bf16)
    dup = pltpu.VMEM((rows, MC, 128), f32)
    dupb = pltpu.VMEM((rows, MC, 128), bf16)
    acc = pltpu.VMEM((rows, MC, 128), f32)
    prod = pltpu.VMEM((2 * rows, MC, 128), f32)
    inv = pltpu.SMEM((2 * PEERS,), jnp.int32)
    lhs = pltpu.VMEM((rows, MC, LW), bf16)
    lhs_remote = pltpu.VMEM((rows, MC, 256), bf16)
    mir = pltpu.VMEM((rows, MC, LW), f32)
    unpacked = pltpu.VMEM((rows * 32, 128), f32)
    pairs = pltpu.VMEM((rows, B, 128), f32)

    def whole(shape_):
        return pl.BlockSpec(shape_, lambda g: (0,) * len(shape_))

    blocks = hblocks.transpose(1, 0, 2)
    sources = sources.T
    one_k = (1, rows, B * B)
    idx, message, wd = pl.pallas_call(
        first_message_kernel,
        grid=(2,),
        out_shape=(shape((16, 128), jnp.int32), msg_shape, wd_shape),
        in_specs=[
            SMEM,
            SMEM,
            whole((K, rows)),
            whole((1, 2 * PEERS)),
            whole((1, rows)),
            whole((cols, width)),
            pl.BlockSpec(one_k, lambda g: (g + 1, 0, 0)),
        ],
        out_specs=(whole((16, 128)), whole(msg_shape.shape), whole(wd_shape.shape)),
        scratch_shapes=[unpacked, pairs, dup, prod, inv],
        compiler_params=limit(60),
        name="first_message",
    )(sources, send_rows, sources, send_rows[None], counts[None], vectors, blocks)

    def exchange(message):
        return lax.all_to_all(message, row_axes, split_axis=0, concat_axis=0, tiled=True)

    received = exchange(message)
    local_scratch = [dup, dupb, lhs, mir, acc]
    um, local = pl.pallas_call(
        first_local_kernel,
        grid=(len(LOCAL),),
        out_shape=(shape((rows, B, LW), bf16), shape((cols, width), f32)),
        in_specs=[
            SMEM,
            whole((cols, width)),
            pl.BlockSpec(one_k, lambda g: (jnp.where(g == 0, 0, 2 * g + 2), 0, 0)),
            pl.BlockSpec(one_k, lambda g: (2 * g + 3, 0, 0)),
        ],
        out_specs=(whole((rows, B, LW)), whole((cols, width))),
        scratch_shapes=[unpacked, unpacked, pairs] + local_scratch,
        compiler_params=limit(60),
        name="first_local",
    )(idx, vectors, blocks, blocks)

    def local_part(block):
        return pl.pallas_call(
            local_product,
            out_shape=shape((cols, width), f32),
            in_specs=[SMEM, VM, VM],
            out_specs=VM,
            scratch_shapes=local_scratch,
            compiler_params=limit(60),
            name="local_product",
        )(idx, block, um)

    def next_step(second, received, local, previous):
        return pl.pallas_call(
            lambda *refs: step_kernel(second, *refs),
            out_shape=(shape((cols, width), bf16), msg_shape),
            in_specs=[SMEM] + [VM] * 5,
            out_specs=(VM, VM),
            scratch_shapes=[lhs_remote, acc, dup, prod, inv],
            compiler_params=limit(60),
            name="second_step" if second else "first_step",
        )(idx, received, local, vectors, previous, wd)

    first, message = next_step(False, received, local, vectors)
    received = exchange(message)
    local = local_part(first)
    filtered, message = next_step(True, received, local, first)
    received = exchange(message)
    local = local_part(filtered)
    own = [filtered] + [
        lax.ppermute(filtered, "y", [(y, (y + d) % NY) for y in range(NY)]) for d in range(1, NY)
    ]
    other = [lax.ppermute(block, "c", [(0, 1), (1, 0)]) for block in own]
    part = pl.pallas_call(
        image_kernel,
        out_shape=shape((NZ, 2 * MC, NY * NC * MC), bf16),
        in_specs=[SMEM] + [VM] * (3 + 2 * NY),
        out_specs=VM,
        scratch_shapes=[
            lhs_remote,
            acc,
            pltpu.VMEM((2 * MC, width), bf16),
            pltpu.VMEM((NY * NC * MC, width), bf16),
        ],
        compiler_params=limit(60),
        name="image",
    )(idx, received, local, wd, *own, *other)
    part = lax.all_to_all(part, "z", split_axis=0, concat_axis=0, tiled=True)
    part = pl.pallas_call(
        sum_z_kernel,
        out_shape=shape((NX,) + part.shape[1:], bf16),
        compiler_params=limit(4),
        name="sum_z",
    )(part)
    part = lax.all_to_all(part, "x", split_axis=0, concat_axis=0, tiled=True)
    gram, projected = pl.pallas_call(
        sum_x_kernel,
        out_shape=(shape((MC, NY * NC * MC), f32),) * 2,
        compiler_params=limit(4),
        name="sum_x",
    )(part)
    return filtered, gram.T, projected.T


def solution(mesh):
    axes = Mesh(mesh.devices.reshape(NZ, NX, NY, NC), ("z", "x", "y", "c"))
    row, col = ("z", "x"), ("y", "c")
    return jax.shard_map(
        on_device,
        mesh=axes,
        in_specs=(P(col, row), P(row, None, None), P(row), P(row, None), P(row)),
        out_specs=(P(col, row), P(None, col), P(None, col)),
        check_vma=False,
    )
```

```python
import jax
import jax.numpy as jnp
from jax import lax
from jax.experimental import pallas as pl
from jax.experimental.pallas import tpu as pltpu
from jax.sharding import Mesh, PartitionSpec as P

B = 64
K = 12
RB = 32
MC = 32
PEERS = 32
NZ, NX, NY, NC = 8, 4, 4, 2
STRIDE = 40
ROOM = 1024
TABLE = 8192
LOCAL = ((0, 3), (4, 5), (6, 7), (8, 9), (10, 11))
LW = 128 * len(LOCAL)
center_value = 0.25
half_width = 1.5
bf16 = jnp.bfloat16
f32 = jnp.float32
MIB = 1024 * 1024

NN = (((1,), (0,)), ((), ()))
NT = (((1,), (1,)), ((), ()))


def low_half(rows=MC):
    return lax.broadcasted_iota(jnp.int32, (rows, 128), 1) < B


def dot(a, b, dims):
    return lax.dot_general(a, b, dims, preferred_element_type=f32)


def store_pair(even_odd_ref, first, second, low):
    even_odd_ref[pl.ds(0, 32, stride=2), :] = jnp.where(low, first, pltpu.roll(second, B, 1))
    even_odd_ref[pl.ds(1, 32, stride=2), :] = jnp.where(low, pltpu.roll(first, B, 1), second)


def duplicate(tile, low):
    turned = pltpu.roll(tile, B, 1)
    return jnp.where(low, tile, turned), jnp.where(low, turned, tile)


def emit_picks(msg_ref, dup_ref, send, low):
    for q in range(PEERS):
        msg_ref[q, 0:MC, :] = jnp.where(
            low, dup_ref[send(2 * q)], dup_ref[send(2 * q + 1)]
        ).astype(bf16)


def emit_mirror(msg_ref, prod_ref, inv_ref, low):
    for q in range(PEERS):
        msg_ref[q, MC : 2 * MC, :] = jnp.where(
            low, prod_ref[inv_ref[2 * q]], prod_ref[inv_ref[2 * q + 1]]
        ).astype(bf16)


def invert_slots(inv_ref, src_ref):
    for i in range(RB):
        for k in (1, 2):
            inv_ref[src_ref[k, i] - RB] = 2 * i + k - 1


def mirror_products(dup_ref, wd_ref, prod_ref):
    for i in range(RB):
        prod = dot(dup_ref[i][:, 0:B].astype(bf16), wd_ref[i], NN)
        prod_ref[2 * i] = prod[:, 0:128]
        prod_ref[2 * i + 1] = prod[:, 128:256]


def starter(sems):
    taken = iter(range(sems.shape[0]))

    def start(source, target):
        copy = pltpu.make_async_copy(source, target, sems.at[next(taken)])
        copy.start()
        return copy

    return start


def unpack_rows(rows_ref, hb_ref):
    for j in range(32):
        rows_ref[STRIDE * j : STRIDE * j + 32, :] = hb_ref[:, 128 * j : 128 * (j + 1)].astype(f32)


def unpacked_row(rows_ref, i):
    return rows_ref[pl.ds(i, 32, stride=STRIDE), :]


def first_message_kernel(src_hbm, send_hbm, v_hbm, hb_hbm, msg_hbm, wd_hbm, table_hbm, keep_hbm, src_ref, send_ref, srcv_ref, sendv_ref, table_ref, v_ref, hb_ref, msg_ref, wd_ref, rows_ref, pair_ref, dup_ref, prod_ref, inv_ref, sems):
    low = low_half()
    start = starter(sems)
    blocks = [start(hb_hbm.at[k], hb_ref.at[k - 1]) for k in (1, 2)]
    vectors = start(v_hbm, v_ref)
    send = start(send_hbm, send_ref)
    src = start(src_hbm, src_ref)
    tables = [start(src_hbm, srcv_ref), start(send_hbm, sendv_ref)]
    vectors.wait()
    keep_out = start(v_ref, keep_hbm.at[0:MC, :])
    for t in range(RB // 2):
        tile = v_ref[:, 128 * t : 128 * (t + 1)].astype(f32)
        dup_ref[2 * t], dup_ref[2 * t + 1] = duplicate(tile, low)
    send.wait()
    emit_picks(msg_ref, dup_ref, lambda c: send_ref[0, c], low)
    picks_out = start(msg_ref.at[:, 0:MC, :], msg_hbm.at[:, 0:MC, :])
    for copy in tables:
        copy.wait()
    table_ref[...] = jnp.zeros(table_ref.shape, jnp.int32)
    table_ref[0:K, 0:RB] = srcv_ref[...]
    table_ref[K : K + 1, 0 : 2 * PEERS] = sendv_ref[...]
    table_out = start(table_ref, table_hbm.at[0:16, :])
    src.wait()
    invert_slots(inv_ref, src_ref)
    for k in (1, 2):
        blocks[k - 1].wait()
        unpack_rows(rows_ref.at[k - 1], hb_ref.at[k - 1])
        for i in range(RB):
            block = unpacked_row(rows_ref.at[k - 1], i)
            pair = pair_ref.at[k - 1, i]
            store_pair(pair, block, block, low)
            wd_ref[i, :, 128 * (k - 1) : 128 * k] = pair[...].astype(bf16)
    weights_out = start(wd_ref, wd_hbm.at[0:RB])
    mirror_products(dup_ref, wd_ref, prod_ref)
    emit_mirror(msg_ref, prod_ref, inv_ref, low)
    mirror_out = start(msg_ref.at[:, MC : 2 * MC, :], msg_hbm.at[:, MC : 2 * MC, :])
    for copy in (keep_out, table_out, picks_out, weights_out, mirror_out):
        copy.wait()


def local_sums(src_ref, v_ref, um_ref, um_ready, y_ref, dup_ref, dupb_ref, lhs_ref, mir_ref, acc_ref):
    low = low_half()
    for t in range(RB // 2):
        tile = v_ref[:, 128 * t : 128 * (t + 1)].astype(f32)
        one, two = duplicate(tile, low)
        dup_ref[2 * t], dup_ref[2 * t + 1] = one, two
        dupb_ref[2 * t], dupb_ref[2 * t + 1] = one.astype(bf16), two.astype(bf16)

    def gather(i, _):
        for t, (k0, k1) in enumerate(LOCAL):
            j0 = i if k0 == 0 else jnp.minimum(src_ref[k0, i], RB - 1)
            j1 = jnp.minimum(src_ref[k1, i], RB - 1)
            lhs_ref[i, :, 128 * t : 128 * (t + 1)] = jnp.where(low, dup_ref[j0], dup_ref[j1]).astype(bf16)
        return 0

    lax.fori_loop(0, RB, gather, 0, unroll=4)
    um_ready()
    for i in range(RB):
        mir_ref[i] = dot(dupb_ref[i][:, 0:B], um_ref[i], NN)
    for i in range(RB):
        acc_ref[i, :, 0:B] = dot(lhs_ref[i], um_ref[i], NT)
        acc_ref[i, :, B:128] = jnp.zeros((MC, B), f32)

    def scatter(i, _):
        for t, (k0, k1) in enumerate(LOCAL):
            j0 = i if k0 == 0 else jnp.minimum(src_ref[k0, i], RB - 1)
            j1 = jnp.minimum(src_ref[k1, i], RB - 1)
            part = mir_ref[i, :, 128 * t : 128 * (t + 1)]
            acc_ref[j0] += jnp.where(low, part, 0.0)
            acc_ref[j1] += jnp.where(low, 0.0, part)
        return 0

    lax.fori_loop(0, RB, scatter, 0, unroll=4)
    for t in range(RB // 2):
        y_ref[:, 128 * t : 128 * (t + 1)] = folded(acc_ref, t, low)


def first_local_kernel(src_hbm, counts_hbm, v_hbm, hb_hbm, um_hbm, y_hbm, src_ref, counts_ref, v_ref, hb_ref, um_ref, y_ref, rows_ref, pair_ref, dup_ref, dupb_ref, lhs_ref, mir_ref, acc_ref, sems, hb_sems):
    low = low_half()
    start = starter(sems)
    counts = start(counts_hbm, counts_ref)

    def block_copies(t):
        k0, k1 = jnp.where(t == 0, 0, 2 * t + 2), 2 * t + 3
        return (
            pltpu.make_async_copy(hb_hbm.at[k0], hb_ref.at[2 * t], hb_sems.at[2 * t]),
            pltpu.make_async_copy(hb_hbm.at[k1], hb_ref.at[2 * t + 1], hb_sems.at[2 * t + 1]),
        )

    for t in range(len(LOCAL)):
        for copy in block_copies(t):
            copy.start()
    src = start(src_hbm, src_ref)
    vectors = start(v_hbm, v_ref)
    counts.wait()

    def relayout(t, _):
        for copy in block_copies(t):
            copy.wait()
        unpack_rows(rows_ref.at[0], hb_ref.at[2 * t])
        unpack_rows(rows_ref.at[1], hb_ref.at[2 * t + 1])
        k0, k1 = jnp.where(t == 0, 0, 2 * t + 2), 2 * t + 3
        lanes = pl.ds(pl.multiple_of(t * 128, 128), 128)
        for i in range(RB):
            count = counts_ref[i]
            one = jnp.where(k0 < count, unpacked_row(rows_ref.at[0], i), 0.0)
            two = jnp.where(k1 < count, unpacked_row(rows_ref.at[1], i), 0.0)
            store_pair(pair_ref.at[i], one, two, low)
            um_ref[i, :, lanes] = pair_ref[i].astype(bf16)
        return 0

    lax.fori_loop(0, len(LOCAL), relayout, 0)
    um_out = start(um_ref, um_hbm)
    src.wait()
    vectors.wait()
    local_sums(src_ref, v_ref, um_ref, lambda: None, y_ref, dup_ref, dupb_ref, lhs_ref, mir_ref, acc_ref)
    y_out = start(y_ref, y_hbm.at[0:MC, :])
    um_out.wait()
    y_out.wait()


def local_kernel(src_hbm, v_hbm, um_hbm, y_hbm, src_ref, v_ref, um_ref, y_ref, dup_ref, dupb_ref, lhs_ref, mir_ref, acc_ref, sems):
    start = starter(sems)
    vectors = start(v_hbm.at[0:MC, :], v_ref)
    src = start(src_hbm, src_ref)
    um = start(um_hbm, um_ref)
    vectors.wait()
    src.wait()
    local_sums(src_ref, v_ref, um_ref, um.wait, y_ref, dup_ref, dupb_ref, lhs_ref, mir_ref, acc_ref)
    start(y_ref, y_hbm.at[0:MC, :]).wait()


def remote_sum(table_ref, recv_ref, wd_ref, wd_ready, lhs_ref, acc_ref):
    low = low_half()
    lane = lax.broadcasted_iota(jnp.int32, (MC, 128), 1) // B

    def gather(i, _):
        for k in (1, 2):
            s = table_ref[k, i] - RB
            tile = recv_ref[s // 2, 0:MC, :].astype(f32)
            lhs_ref[i, :, 128 * (k - 1) : 128 * k] = jnp.where(lane == s % 2, tile, 0.0).astype(bf16)
        return 0

    lax.fori_loop(0, RB, gather, 0, unroll=4)
    wd_ready()
    for i in range(RB):
        acc_ref[i, :, 0:B] = dot(lhs_ref[i], wd_ref[i], NT)
        acc_ref[i, :, B:128] = jnp.zeros((MC, B), f32)

    def scatter(q, _):
        tile = recv_ref[q, MC : 2 * MC, :].astype(f32)
        acc_ref[table_ref[K, 2 * q]] += jnp.where(low, tile, 0.0)
        acc_ref[table_ref[K, 2 * q + 1]] += jnp.where(low, 0.0, tile)
        return 0

    lax.fori_loop(0, PEERS, scatter, 0, unroll=4)


def folded(acc_ref, t, low):
    one, two = acc_ref[2 * t], acc_ref[2 * t + 1]
    return jnp.where(low, one + pltpu.roll(one, B, 1), two + pltpu.roll(two, B, 1))


def step_kernel(second, table_hbm, recv_ref, y_hbm, v_hbm, prev_hbm, wd_hbm, out_hbm, msg_hbm, table_ref, y_ref, v_ref, prev_ref, wd_ref, out_ref, msg_ref, lhs_ref, acc_ref, dup_ref, prod_ref, inv_ref, sems):
    low = low_half()
    start = starter(sems)
    table = start(table_hbm.at[0:16, :], table_ref)
    wd = start(wd_hbm.at[0:RB], wd_ref)
    terms = [start(y_hbm.at[0:MC, :], y_ref), start(v_hbm.at[0:MC, :], v_ref)]
    if second:
        terms.append(start(prev_hbm.at[0:MC, :], prev_ref))
    table.wait()
    invert_slots(inv_ref, table_ref)
    remote_sum(table_ref, recv_ref, wd_ref, wd.wait, lhs_ref, acc_ref)
    for copy in terms:
        copy.wait()
    for t in range(RB // 2):
        lanes = slice(128 * t, 128 * (t + 1))
        image = folded(acc_ref, t, low) + y_ref[:, lanes]
        if second:
            tile = 2.0 * (image - center_value * prev_ref[:, lanes].astype(f32)) / half_width - v_ref[:, lanes].astype(f32)
        else:
            tile = (image - center_value * v_ref[:, lanes].astype(f32)) / half_width
        tile = tile.astype(bf16)
        out_ref[:, lanes] = tile
        dup_ref[2 * t], dup_ref[2 * t + 1] = duplicate(tile.astype(f32), low)
    result_out = start(out_ref, out_hbm.at[0:MC, :])
    emit_picks(msg_ref, dup_ref, lambda c: table_ref[K, c], low)
    picks_out = start(msg_ref.at[:, 0:MC, :], msg_hbm.at[:, 0:MC, :])
    mirror_products(dup_ref, wd_ref, prod_ref)
    emit_mirror(msg_ref, prod_ref, inv_ref, low)
    mirror_out = start(msg_ref.at[:, MC : 2 * MC, :], msg_hbm.at[:, MC : 2 * MC, :])
    result_out.wait()
    picks_out.wait()
    mirror_out.wait()


def image_kernel(table_hbm, recv_ref, y_hbm, wd_hbm, *refs):
    own, other = refs[0:NY], refs[NY : 2 * NY]
    out_ref, table_ref, y_ref, wd_ref, lhs_ref, acc_ref, stack_ref, all_ref, sems = refs[2 * NY :]
    low = low_half()
    start = starter(sems)
    table = start(table_hbm.at[0:16, :], table_ref)
    wd = start(wd_hbm.at[0:RB], wd_ref)
    y_sum = start(y_hbm.at[0:MC, :], y_ref)
    y, c = lax.axis_index("y"), lax.axis_index("c")
    moves = [start(own[0], stack_ref.at[0:MC, :])]
    for d in range(NY):
        from_y = lax.rem(y + NY - d, NY) * NC
        for block, core in ((own[d], c), (other[d], 1 - c)):
            moves.append(start(block, all_ref.at[pl.ds(pl.multiple_of((from_y + core) * MC, MC), MC), :]))
    table.wait()
    remote_sum(table_ref, recv_ref, wd_ref, wd.wait, lhs_ref, acc_ref)
    y_sum.wait()
    for t in range(RB // 2):
        lanes = slice(128 * t, 128 * (t + 1))
        stack_ref[MC : 2 * MC, lanes] = (folded(acc_ref, t, low) + y_ref[:, lanes]).astype(bf16)
    for copy in moves:
        copy.wait()
    part = dot(stack_ref[...], all_ref[...], NT).astype(bf16)
    for z in range(NZ):
        out_ref[z] = part


def sum_z_kernel(in_ref, out_ref):
    total = in_ref[0].astype(f32)
    for z in range(1, NZ):
        total = total + in_ref[z].astype(f32)
    total = total.astype(bf16)
    for x in range(NX):
        out_ref[x] = total


def sum_x_kernel(in_ref, gram_ref, proj_ref):
    total = in_ref[0].astype(f32)
    for x in range(1, NX):
        total = total + in_ref[x].astype(f32)
    gram_ref[...] = total[0:MC, :]
    proj_ref[...] = total[MC : 2 * MC, :]


VM = pl.BlockSpec(memory_space=pltpu.VMEM)
ANY = pl.BlockSpec(memory_space=pl.ANY)
HBM = pl.BlockSpec(memory_space=pltpu.HBM)
shape = jax.ShapeDtypeStruct


def limit(mib):
    return pltpu.CompilerParams(vmem_limit_bytes=int(mib * MIB))


def semaphores(count):
    return pltpu.SemaphoreType.DMA((count,))


def on_device(vectors, hblocks, counts, sources, send_rows):
    cols, width = vectors.shape
    row_axes, rows = ("z", "x"), hblocks.shape[0]
    msg_shape = shape((PEERS, 2 * MC, 128), bf16)
    um_shape = shape((rows, B, LW), bf16)
    vec = pltpu.VMEM((cols, width), bf16)
    vec_sum = pltpu.VMEM((cols, width), f32)
    msg = pltpu.VMEM(msg_shape.shape, bf16)
    wd_scratch = pltpu.VMEM((rows, B, 256), bf16)
    um_scratch = pltpu.VMEM(um_shape.shape, bf16)
    dup = pltpu.VMEM((rows, MC, 128), f32)
    dupb = pltpu.VMEM((rows, MC, 128), bf16)
    acc = pltpu.VMEM((rows, MC, 128), f32)
    prod = pltpu.VMEM((2 * rows, MC, 128), f32)
    inv = pltpu.SMEM((2 * PEERS,), jnp.int32)
    src = pltpu.SMEM((K, rows), jnp.int32)
    table_scratch = pltpu.SMEM((16, 128), jnp.int32)
    lhs = pltpu.VMEM((rows, MC, LW), bf16)
    lhs_remote = pltpu.VMEM((rows, MC, 256), bf16)
    mir = pltpu.VMEM((rows, MC, LW), f32)
    unpacked = pltpu.VMEM((2, STRIDE * 32, 128), f32)

    blocks = hblocks.transpose(1, 0, 2)
    sources = sources.T
    message, wd, table, kept = pl.pallas_call(
        first_message_kernel,
        out_shape=(
            msg_shape,
            shape((4 * rows, B, 256), bf16),
            shape((TABLE, 128), jnp.int32),
            shape((ROOM, width), bf16),
        ),
        in_specs=[HBM] * 4,
        out_specs=(HBM,) * 4,
        scratch_shapes=[
            src,
            pltpu.SMEM((1, 2 * PEERS), jnp.int32),
            pltpu.VMEM((K, rows), jnp.int32),
            pltpu.VMEM((1, 2 * PEERS), jnp.int32),
            pltpu.VMEM((16, 128), jnp.int32),
            vec,
            pltpu.VMEM((2, rows, B * B), bf16),
            msg,
            wd_scratch,
            unpacked,
            pltpu.VMEM((2, rows, B, 128), f32),
            dup,
            prod,
            inv,
            semaphores(12),
        ],
        compiler_params=limit(60),
        name="first_message",
    )(sources, send_rows[None], vectors, blocks)

    def exchange(message):
        return lax.all_to_all(message, row_axes, split_axis=0, concat_axis=0, tiled=True)

    received = exchange(message)
    local_scratch = [dup, dupb, lhs, mir, acc]
    um, local = pl.pallas_call(
        first_local_kernel,
        out_shape=(um_shape, shape((ROOM, width), f32)),
        in_specs=[HBM] * 4,
        out_specs=(HBM, HBM),
        scratch_shapes=[
            src,
            pltpu.SMEM((rows,), jnp.int32),
            vec,
            pltpu.VMEM((2 * len(LOCAL), rows, B * B), bf16),
            um_scratch,
            vec_sum,
            unpacked,
            pltpu.VMEM((rows, B, 128), f32),
        ]
        + local_scratch
        + [semaphores(5), semaphores(2 * len(LOCAL))],
        compiler_params=limit(60),
        name="first_local",
    )(sources, counts, vectors, blocks)

    def local_part(block):
        return pl.pallas_call(
            local_kernel,
            out_shape=shape((ROOM, width), f32),
            in_specs=[HBM] * 3,
            out_specs=HBM,
            scratch_shapes=[src, vec, um_scratch, vec_sum] + local_scratch + [semaphores(4)],
            compiler_params=limit(60),
            name="local_product",
        )(sources, block, um)

    def next_step(second, received, local, previous):
        return pl.pallas_call(
            lambda *refs: step_kernel(second, *refs),
            out_shape=(shape((cols if second else ROOM, width), bf16), msg_shape),
            in_specs=[HBM, VM] + [HBM] * 4,
            out_specs=(HBM, HBM),
            scratch_shapes=[table_scratch, vec_sum, vec, vec, wd_scratch, vec, msg, lhs_remote, acc, dup, prod, inv]
            + [semaphores(9)],
            compiler_params=limit(51.6),
            name="second_step" if second else "first_step",
        )(table, received, local, kept, previous, wd)

    first, message = next_step(False, received, local, kept)
    received = exchange(message)
    local = local_part(first)
    filtered, message = next_step(True, received, local, first)
    received = exchange(message)
    local = local_part(filtered)
    own = [filtered] + [
        lax.ppermute(filtered, "y", [(y, (y + d) % NY) for y in range(NY)]) for d in range(1, NY)
    ]
    other = [lax.ppermute(block, "c", [(0, 1), (1, 0)]) for block in own]
    part = pl.pallas_call(
        image_kernel,
        out_shape=shape((NZ, 2 * MC, NY * NC * MC), bf16),
        in_specs=[HBM, VM, HBM, HBM, HBM] + [ANY] * (2 * NY - 1),
        out_specs=VM,
        scratch_shapes=[
            table_scratch,
            vec_sum,
            wd_scratch,
            lhs_remote,
            acc,
            pltpu.VMEM((2 * MC, width), bf16),
            pltpu.VMEM((NY * NC * MC, width), bf16),
            semaphores(5 + 2 * NY),
        ],
        compiler_params=limit(51.6),
        name="image",
    )(table, received, local, wd, *own, *other)
    part = lax.all_to_all(part, "z", split_axis=0, concat_axis=0, tiled=True)
    part = pl.pallas_call(
        sum_z_kernel,
        out_shape=shape((NX,) + part.shape[1:], bf16),
        compiler_params=limit(4),
        name="sum_z",
    )(part)
    part = lax.all_to_all(part, "x", split_axis=0, concat_axis=0, tiled=True)
    gram, projected = pl.pallas_call(
        sum_x_kernel,
        out_shape=(shape((MC, NY * NC * MC), f32),) * 2,
        compiler_params=limit(4),
        name="sum_x",
    )(part)
    return filtered, gram.T, projected.T


def solution(mesh):
    axes = Mesh(mesh.devices.reshape(NZ, NX, NY, NC), ("z", "x", "y", "c"))
    row, col = ("z", "x"), ("y", "c")
    return jax.shard_map(
        on_device,
        mesh=axes,
        in_specs=(P(col, row), P(row, None, None), P(row), P(row, None), P(row)),
        out_specs=(P(col, row), P(None, col), P(None, col)),
        check_vma=False,
    )
```

```python
import jax
import jax.numpy as jnp
from jax import lax
from jax.experimental import pallas as pl
from jax.experimental.pallas import tpu as pltpu
from jax.sharding import Mesh, PartitionSpec as P

B = 64
K = 12
RB = 32
MC = 32
PEERS = 32
NZ, NX, NY, NC = 8, 4, 4, 2
STRIDE = 40
ROOM = 1024
TABLE = 8192
LOCAL = ((0, 3), (4, 5), (6, 7), (8, 9), (10, 11))
LW = 128 * len(LOCAL)
center_value = 0.25
half_width = 1.5
bf16 = jnp.bfloat16
f32 = jnp.float32
MIB = 1024 * 1024

NN = (((1,), (0,)), ((), ()))
NT = (((1,), (1,)), ((), ()))


def low_half(rows=MC):
    return lax.broadcasted_iota(jnp.int32, (rows, 128), 1) < B


def dot(a, b, dims):
    return lax.dot_general(a, b, dims, preferred_element_type=f32)


def store_pair(even_odd_ref, first, second, low):
    even_odd_ref[pl.ds(0, 32, stride=2), :] = jnp.where(low, first, pltpu.roll(second, B, 1))
    even_odd_ref[pl.ds(1, 32, stride=2), :] = jnp.where(low, pltpu.roll(first, B, 1), second)


def duplicate(tile, low):
    turned = pltpu.roll(tile, B, 1)
    return jnp.where(low, tile, turned), jnp.where(low, turned, tile)


def emit_picks(msg_ref, dup_ref, send, low):
    for q in range(PEERS):
        msg_ref[q, 0:MC, :] = jnp.where(
            low, dup_ref[send(2 * q)], dup_ref[send(2 * q + 1)]
        ).astype(bf16)


def emit_mirror(msg_ref, prod_ref, inv_ref, low):
    for q in range(PEERS):
        msg_ref[q, MC : 2 * MC, :] = jnp.where(
            low, prod_ref[inv_ref[2 * q]], prod_ref[inv_ref[2 * q + 1]]
        ).astype(bf16)


def invert_slots(inv_ref, src_ref):
    for i in range(RB):
        for k in (1, 2):
            inv_ref[src_ref[k, i] - RB] = 2 * i + k - 1


def mirror_products(dup_ref, wd_ref, prod_ref):
    for i in range(RB):
        prod = dot(dup_ref[i][:, 0:B].astype(bf16), wd_ref[i], NN)
        prod_ref[2 * i] = prod[:, 0:128]
        prod_ref[2 * i + 1] = prod[:, 128:256]


def starter(sems):
    taken = iter(range(sems.shape[0]))

    def start(source, target):
        copy = pltpu.make_async_copy(source, target, sems.at[next(taken)])
        copy.start()
        return copy

    return start


def unpack_rows(rows_ref, hb_ref):
    for j in range(32):
        rows_ref[STRIDE * j : STRIDE * j + 32, :] = hb_ref[:, 128 * j : 128 * (j + 1)].astype(f32)


def unpacked_row(rows_ref, i):
    return rows_ref[pl.ds(i, 32, stride=STRIDE), :]


def first_message_kernel(src_hbm, send_hbm, v_hbm, hb_hbm, msg_hbm, wd_hbm, table_hbm, keep_hbm, src_ref, send_ref, srcv_ref, sendv_ref, table_ref, v_ref, hb_ref, msg_ref, wd_ref, rows_ref, pair_ref, dup_ref, prod_ref, inv_ref, sems):
    low = low_half()
    start = starter(sems)
    blocks = [start(hb_hbm.at[k], hb_ref.at[k - 1]) for k in (1, 2)]
    vectors = start(v_hbm, v_ref)
    send = start(send_hbm, send_ref)
    src = start(src_hbm, src_ref)
    tables = [start(src_hbm, srcv_ref), start(send_hbm, sendv_ref)]
    vectors.wait()
    keep_out = start(v_ref, keep_hbm.at[0:MC, :])
    for t in range(RB // 2):
        tile = v_ref[:, 128 * t : 128 * (t + 1)].astype(f32)
        dup_ref[2 * t], dup_ref[2 * t + 1] = duplicate(tile, low)
    send.wait()
    emit_picks(msg_ref, dup_ref, lambda c: send_ref[0, c], low)
    picks_out = start(msg_ref.at[:, 0:MC, :], msg_hbm.at[:, 0:MC, :])
    for copy in tables:
        copy.wait()
    table_ref[...] = jnp.zeros(table_ref.shape, jnp.int32)
    table_ref[0:K, 0:RB] = srcv_ref[...]
    table_ref[K : K + 1, 0 : 2 * PEERS] = sendv_ref[...]
    table_out = start(table_ref, table_hbm.at[0:16, :])
    src.wait()
    invert_slots(inv_ref, src_ref)
    for k in (1, 2):
        blocks[k - 1].wait()
        unpack_rows(rows_ref.at[k - 1], hb_ref.at[k - 1])
        for i in range(RB):
            block = unpacked_row(rows_ref.at[k - 1], i)
            pair = pair_ref.at[k - 1, i]
            store_pair(pair, block, block, low)
            wd_ref[i, :, 128 * (k - 1) : 128 * k] = pair[...].astype(bf16)
    weights_out = start(wd_ref, wd_hbm.at[0:RB])
    mirror_products(dup_ref, wd_ref, prod_ref)
    emit_mirror(msg_ref, prod_ref, inv_ref, low)
    mirror_out = start(msg_ref.at[:, MC : 2 * MC, :], msg_hbm.at[:, MC : 2 * MC, :])
    for copy in (keep_out, table_out, picks_out, weights_out, mirror_out):
        copy.wait()


def local_sums(src_ref, v_ref, um_ref, um_ready, y_ref, dup_ref, dupb_ref, lhs_ref, mir_ref, acc_ref):
    low = low_half()
    for t in range(RB // 2):
        tile = v_ref[:, 128 * t : 128 * (t + 1)].astype(f32)
        one, two = duplicate(tile, low)
        dup_ref[2 * t], dup_ref[2 * t + 1] = one, two
        dupb_ref[2 * t], dupb_ref[2 * t + 1] = one.astype(bf16), two.astype(bf16)

    def gather(i, _):
        for t, (k0, k1) in enumerate(LOCAL):
            j0 = i if k0 == 0 else jnp.minimum(src_ref[k0, i], RB - 1)
            j1 = jnp.minimum(src_ref[k1, i], RB - 1)
            lhs_ref[i, :, 128 * t : 128 * (t + 1)] = jnp.where(low, dup_ref[j0], dup_ref[j1]).astype(bf16)
        return 0

    lax.fori_loop(0, RB, gather, 0, unroll=4)
    um_ready()
    for i in range(RB):
        mir_ref[i] = dot(dupb_ref[i][:, 0:B], um_ref[i], NN)
    for i in range(RB):
        acc_ref[i, :, 0:B] = dot(lhs_ref[i], um_ref[i], NT)
        acc_ref[i, :, B:128] = jnp.zeros((MC, B), f32)

    def scatter(i, _):
        for t, (k0, k1) in enumerate(LOCAL):
            j0 = i if k0 == 0 else jnp.minimum(src_ref[k0, i], RB - 1)
            j1 = jnp.minimum(src_ref[k1, i], RB - 1)
            part = mir_ref[i, :, 128 * t : 128 * (t + 1)]
            acc_ref[j0] += jnp.where(low, part, 0.0)
            acc_ref[j1] += jnp.where(low, 0.0, part)
        return 0

    lax.fori_loop(0, RB, scatter, 0, unroll=4)
    for t in range(RB // 2):
        y_ref[:, 128 * t : 128 * (t + 1)] = folded(acc_ref, t, low)


def first_local_kernel(src_hbm, counts_hbm, v_hbm, hb_hbm, um_hbm, y_hbm, src_ref, counts_ref, v_ref, hb_ref, um_ref, y_ref, rows_ref, pair_ref, dup_ref, dupb_ref, lhs_ref, mir_ref, acc_ref, sems, hb_sems):
    low = low_half()
    start = starter(sems)
    counts = start(counts_hbm, counts_ref)

    def block_copies(t):
        k0, k1 = jnp.where(t == 0, 0, 2 * t + 2), 2 * t + 3
        return (
            pltpu.make_async_copy(hb_hbm.at[k0], hb_ref.at[2 * t], hb_sems.at[2 * t]),
            pltpu.make_async_copy(hb_hbm.at[k1], hb_ref.at[2 * t + 1], hb_sems.at[2 * t + 1]),
        )

    for t in range(len(LOCAL)):
        for copy in block_copies(t):
            copy.start()
    src = start(src_hbm, src_ref)
    vectors = start(v_hbm, v_ref)
    counts.wait()

    def relayout(t, _):
        for copy in block_copies(t):
            copy.wait()
        unpack_rows(rows_ref.at[0], hb_ref.at[2 * t])
        unpack_rows(rows_ref.at[1], hb_ref.at[2 * t + 1])
        k0, k1 = jnp.where(t == 0, 0, 2 * t + 2), 2 * t + 3
        lanes = pl.ds(pl.multiple_of(t * 128, 128), 128)
        for i in range(RB):
            count = counts_ref[i]
            one = jnp.where(k0 < count, unpacked_row(rows_ref.at[0], i), 0.0)
            two = jnp.where(k1 < count, unpacked_row(rows_ref.at[1], i), 0.0)
            store_pair(pair_ref.at[i], one, two, low)
            um_ref[i, :, lanes] = pair_ref[i].astype(bf16)
        return 0

    lax.fori_loop(0, len(LOCAL), relayout, 0)
    um_out = start(um_ref, um_hbm)
    src.wait()
    vectors.wait()
    local_sums(src_ref, v_ref, um_ref, lambda: None, y_ref, dup_ref, dupb_ref, lhs_ref, mir_ref, acc_ref)
    y_out = start(y_ref, y_hbm.at[0:MC, :])
    um_out.wait()
    y_out.wait()


def local_kernel(src_hbm, v_hbm, um_hbm, y_hbm, src_ref, v_ref, um_ref, y_ref, dup_ref, dupb_ref, lhs_ref, mir_ref, acc_ref, sems):
    start = starter(sems)
    vectors = start(v_hbm.at[0:MC, :], v_ref)
    src = start(src_hbm, src_ref)
    um = start(um_hbm, um_ref)
    vectors.wait()
    src.wait()
    local_sums(src_ref, v_ref, um_ref, um.wait, y_ref, dup_ref, dupb_ref, lhs_ref, mir_ref, acc_ref)
    start(y_ref, y_hbm.at[0:MC, :]).wait()


def remote_sum(table_ref, recv_ref, wd_ref, wd_ready, lhs_ref, acc_ref):
    low = low_half()
    lane = lax.broadcasted_iota(jnp.int32, (MC, 128), 1) // B

    def gather(i, _):
        for k in (1, 2):
            s = table_ref[k, i] - RB
            tile = recv_ref[s // 2, 0:MC, :].astype(f32)
            lhs_ref[i, :, 128 * (k - 1) : 128 * k] = jnp.where(lane == s % 2, tile, 0.0).astype(bf16)
        return 0

    lax.fori_loop(0, RB, gather, 0, unroll=4)
    wd_ready()
    for i in range(RB):
        acc_ref[i, :, 0:B] = dot(lhs_ref[i], wd_ref[i], NT)
        acc_ref[i, :, B:128] = jnp.zeros((MC, B), f32)

    def scatter(q, _):
        tile = recv_ref[q, MC : 2 * MC, :].astype(f32)
        acc_ref[table_ref[K, 2 * q]] += jnp.where(low, tile, 0.0)
        acc_ref[table_ref[K, 2 * q + 1]] += jnp.where(low, 0.0, tile)
        return 0

    lax.fori_loop(0, PEERS, scatter, 0, unroll=4)


def folded(acc_ref, t, low):
    one, two = acc_ref[2 * t], acc_ref[2 * t + 1]
    return jnp.where(low, one + pltpu.roll(one, B, 1), two + pltpu.roll(two, B, 1))


def step_kernel(second, table_hbm, recv_ref, y_hbm, v_hbm, prev_hbm, wd_hbm, out_hbm, msg_hbm, table_ref, y_ref, v_ref, prev_ref, wd_ref, out_ref, msg_ref, lhs_ref, acc_ref, dup_ref, prod_ref, inv_ref, sems):
    low = low_half()
    start = starter(sems)
    table = start(table_hbm.at[0:16, :], table_ref)
    wd = start(wd_hbm.at[0:RB], wd_ref)
    terms = [start(y_hbm.at[0:MC, :], y_ref), start(v_hbm.at[0:MC, :], v_ref)]
    if second:
        terms.append(start(prev_hbm.at[0:MC, :], prev_ref))
    table.wait()
    invert_slots(inv_ref, table_ref)
    remote_sum(table_ref, recv_ref, wd_ref, wd.wait, lhs_ref, acc_ref)
    for copy in terms:
        copy.wait()
    for t in range(RB // 2):
        lanes = slice(128 * t, 128 * (t + 1))
        image = folded(acc_ref, t, low) + y_ref[:, lanes]
        if second:
            tile = 2.0 * (image - center_value * prev_ref[:, lanes].astype(f32)) / half_width - v_ref[:, lanes].astype(f32)
        else:
            tile = (image - center_value * v_ref[:, lanes].astype(f32)) / half_width
        tile = tile.astype(bf16)
        out_ref[:, lanes] = tile
        dup_ref[2 * t], dup_ref[2 * t + 1] = duplicate(tile.astype(f32), low)
    result_out = start(out_ref, out_hbm.at[0:MC, :])
    emit_picks(msg_ref, dup_ref, lambda c: table_ref[K, c], low)
    picks_out = start(msg_ref.at[:, 0:MC, :], msg_hbm.at[:, 0:MC, :])
    mirror_products(dup_ref, wd_ref, prod_ref)
    emit_mirror(msg_ref, prod_ref, inv_ref, low)
    mirror_out = start(msg_ref.at[:, MC : 2 * MC, :], msg_hbm.at[:, MC : 2 * MC, :])
    result_out.wait()
    picks_out.wait()
    mirror_out.wait()


def image_kernel(table_hbm, recv_ref, y_hbm, wd_hbm, *refs):
    own, other = refs[0:NY], refs[NY : 2 * NY]
    out_ref, table_ref, y_ref, wd_ref, lhs_ref, acc_ref, stack_ref, all_ref, sems = refs[2 * NY :]
    low = low_half()
    start = starter(sems)
    table = start(table_hbm.at[0:16, :], table_ref)
    wd = start(wd_hbm.at[0:RB], wd_ref)
    y_sum = start(y_hbm.at[0:MC, :], y_ref)
    y, c = lax.axis_index("y"), lax.axis_index("c")
    moves = [start(own[0], stack_ref.at[0:MC, :])]
    for d in range(NY):
        from_y = lax.rem(y + NY - d, NY) * NC
        for block, core in ((own[d], c), (other[d], 1 - c)):
            moves.append(start(block, all_ref.at[pl.ds(pl.multiple_of((from_y + core) * MC, MC), MC), :]))
    table.wait()
    remote_sum(table_ref, recv_ref, wd_ref, wd.wait, lhs_ref, acc_ref)
    y_sum.wait()
    for t in range(RB // 2):
        lanes = slice(128 * t, 128 * (t + 1))
        stack_ref[MC : 2 * MC, lanes] = (folded(acc_ref, t, low) + y_ref[:, lanes]).astype(bf16)
    for copy in moves:
        copy.wait()
    part = dot(stack_ref[...], all_ref[...], NT).astype(bf16)
    for z in range(NZ):
        out_ref[z] = part


def sum_z_kernel(in_ref, out_ref):
    total = in_ref[0].astype(f32)
    for z in range(1, NZ):
        total = total + in_ref[z].astype(f32)
    total = total.astype(bf16)
    for x in range(NX):
        out_ref[x] = total


def sum_x_kernel(in_ref, gram_ref, proj_ref):
    total = in_ref[0].astype(f32)
    for x in range(1, NX):
        total = total + in_ref[x].astype(f32)
    gram_ref[...] = total[0:MC, :]
    proj_ref[...] = total[MC : 2 * MC, :]


VM = pl.BlockSpec(memory_space=pltpu.VMEM)
ANY = pl.BlockSpec(memory_space=pl.ANY)
HBM = pl.BlockSpec(memory_space=pltpu.HBM)
shape = jax.ShapeDtypeStruct


def limit(mib):
    return pltpu.CompilerParams(vmem_limit_bytes=int(mib * MIB))


LOCAL_COST = pl.CostEstimate(flops=2 * 2 * RB * 10 * MC * B * B, bytes_accessed=20 * MIB, transcendentals=0)


def semaphores(count):
    return pltpu.SemaphoreType.DMA((count,))


def on_device(vectors, hblocks, counts, sources, send_rows):
    cols, width = vectors.shape
    row_axes, rows = ("z", "x"), hblocks.shape[0]
    msg_shape = shape((PEERS, 2 * MC, 128), bf16)
    um_shape = shape((rows, B, LW), bf16)
    vec = pltpu.VMEM((cols, width), bf16)
    vec_sum = pltpu.VMEM((cols, width), f32)
    msg = pltpu.VMEM(msg_shape.shape, bf16)
    wd_scratch = pltpu.VMEM((rows, B, 256), bf16)
    um_scratch = pltpu.VMEM(um_shape.shape, bf16)
    dup = pltpu.VMEM((rows, MC, 128), f32)
    dupb = pltpu.VMEM((rows, MC, 128), bf16)
    acc = pltpu.VMEM((rows, MC, 128), f32)
    prod = pltpu.VMEM((2 * rows, MC, 128), f32)
    inv = pltpu.SMEM((2 * PEERS,), jnp.int32)
    src = pltpu.SMEM((K, rows), jnp.int32)
    table_scratch = pltpu.SMEM((16, 128), jnp.int32)
    lhs = pltpu.VMEM((rows, MC, LW), bf16)
    lhs_remote = pltpu.VMEM((rows, MC, 256), bf16)
    mir = pltpu.VMEM((rows, MC, LW), f32)
    unpacked = pltpu.VMEM((2, STRIDE * 32, 128), f32)

    blocks = hblocks.transpose(1, 0, 2)
    sources = sources.T
    message, wd, table, kept = pl.pallas_call(
        first_message_kernel,
        out_shape=(
            msg_shape,
            shape((4 * rows, B, 256), bf16),
            shape((TABLE, 128), jnp.int32),
            shape((ROOM, width), bf16),
        ),
        in_specs=[HBM] * 4,
        out_specs=(HBM,) * 4,
        scratch_shapes=[
            src,
            pltpu.SMEM((1, 2 * PEERS), jnp.int32),
            pltpu.VMEM((K, rows), jnp.int32),
            pltpu.VMEM((1, 2 * PEERS), jnp.int32),
            pltpu.VMEM((16, 128), jnp.int32),
            vec,
            pltpu.VMEM((2, rows, B * B), bf16),
            msg,
            wd_scratch,
            unpacked,
            pltpu.VMEM((2, rows, B, 128), f32),
            dup,
            prod,
            inv,
            semaphores(12),
        ],
        compiler_params=limit(60),
        name="first_message",
    )(sources, send_rows[None], vectors, blocks)

    def exchange(message):
        return lax.all_to_all(message, row_axes, split_axis=0, concat_axis=0, tiled=True)

    received = exchange(message)
    local_scratch = [dup, dupb, lhs, mir, acc]
    um, local = pl.pallas_call(
        first_local_kernel,
        out_shape=(um_shape, shape((ROOM, width), f32)),
        in_specs=[HBM] * 4,
        out_specs=(HBM, HBM),
        scratch_shapes=[
            src,
            pltpu.SMEM((rows,), jnp.int32),
            vec,
            pltpu.VMEM((2 * len(LOCAL), rows, B * B), bf16),
            um_scratch,
            vec_sum,
            unpacked,
            pltpu.VMEM((rows, B, 128), f32),
        ]
        + local_scratch
        + [semaphores(5), semaphores(2 * len(LOCAL))],
        compiler_params=limit(60),
        name="first_local",
    )(sources, counts, vectors, blocks)

    def local_part(block):
        return pl.pallas_call(
            local_kernel,
            out_shape=shape((ROOM, width), f32),
            in_specs=[HBM] * 3,
            out_specs=HBM,
            scratch_shapes=[src, vec, um_scratch, vec_sum] + local_scratch + [semaphores(4)],
            compiler_params=limit(60),
            cost_estimate=LOCAL_COST,
            name="local_product",
        )(sources, block, um)

    def next_step(second, received, local, previous):
        return pl.pallas_call(
            lambda *refs: step_kernel(second, *refs),
            out_shape=(shape((cols if second else ROOM, width), bf16), msg_shape),
            in_specs=[HBM, VM] + [HBM] * 4,
            out_specs=(HBM, HBM),
            scratch_shapes=[table_scratch, vec_sum, vec, vec, wd_scratch, vec, msg, lhs_remote, acc, dup, prod, inv]
            + [semaphores(9)],
            compiler_params=limit(51.6),
            name="second_step" if second else "first_step",
        )(table, received, local, kept, previous, wd)

    first, message = next_step(False, received, local, kept)
    received = exchange(message)
    local = local_part(first)
    filtered, message = next_step(True, received, local, first)
    received = exchange(message)
    local = local_part(filtered)
    own = [filtered] + [
        lax.ppermute(filtered, "y", [(y, (y + d) % NY) for y in range(NY)]) for d in range(1, NY)
    ]
    local, *passed = lax.optimization_barrier((local, *own[1:]))
    own = own[:1] + passed
    other = [lax.ppermute(block, "c", [(0, 1), (1, 0)]) for block in own]
    part = pl.pallas_call(
        image_kernel,
        out_shape=shape((NZ, 2 * MC, NY * NC * MC), bf16),
        in_specs=[HBM, VM, HBM, HBM, HBM] + [ANY] * (2 * NY - 1),
        out_specs=VM,
        scratch_shapes=[
            table_scratch,
            vec_sum,
            wd_scratch,
            lhs_remote,
            acc,
            pltpu.VMEM((2 * MC, width), bf16),
            pltpu.VMEM((NY * NC * MC, width), bf16),
            semaphores(5 + 2 * NY),
        ],
        compiler_params=limit(51.6),
        name="image",
    )(table, received, local, wd, *own, *other)
    part = lax.all_to_all(part, "z", split_axis=0, concat_axis=0, tiled=True)
    part = pl.pallas_call(
        sum_z_kernel,
        out_shape=shape((NX,) + part.shape[1:], bf16),
        compiler_params=limit(4),
        name="sum_z",
    )(part)
    part = lax.all_to_all(part, "x", split_axis=0, concat_axis=0, tiled=True)
    gram, projected = pl.pallas_call(
        sum_x_kernel,
        out_shape=(shape((MC, NY * NC * MC), f32),) * 2,
        compiler_params=limit(4),
        name="sum_x",
    )(part)
    return filtered, gram.T, projected.T


def solution(mesh):
    axes = Mesh(mesh.devices.reshape(NZ, NX, NY, NC), ("z", "x", "y", "c"))
    row, col = ("z", "x"), ("y", "c")
    return jax.shard_map(
        on_device,
        mesh=axes,
        in_specs=(P(col, row), P(row, None, None), P(row), P(row, None), P(row)),
        out_specs=(P(col, row), P(None, col), P(None, col)),
        check_vma=False,
    )
```

```python
import jax
import jax.numpy as jnp
from jax import lax
from jax.experimental import pallas as pl
from jax.experimental.pallas import tpu as pltpu
from jax.sharding import Mesh, PartitionSpec as P

B = 64
K = 12
RB = 32
MC = 32
PEERS = 32
NZ, NX, NY, NC = 8, 4, 4, 2
STRIDE = 40
ROOM = 1024
TABLE = 8192
LOCAL = ((0, 3), (4, 5), (6, 7), (8, 9), (10, 11))
LW = 128 * len(LOCAL)
center_value = 0.25
half_width = 1.5
bf16 = jnp.bfloat16
f32 = jnp.float32
MIB = 1024 * 1024

NN = (((1,), (0,)), ((), ()))
NT = (((1,), (1,)), ((), ()))


def low_half(rows=MC):
    return lax.broadcasted_iota(jnp.int32, (rows, 128), 1) < B


def dot(a, b, dims):
    return lax.dot_general(a, b, dims, preferred_element_type=f32)


def store_pair(even_odd_ref, first, second, low):
    even_odd_ref[pl.ds(0, 32, stride=2), :] = jnp.where(low, first, pltpu.roll(second, B, 1))
    even_odd_ref[pl.ds(1, 32, stride=2), :] = jnp.where(low, pltpu.roll(first, B, 1), second)


def duplicate(tile, low):
    turned = pltpu.roll(tile, B, 1)
    return jnp.where(low, tile, turned), jnp.where(low, turned, tile)


def emit_picks(msg_ref, dup_ref, send, low):
    for q in range(PEERS):
        msg_ref[q, 0:MC, :] = jnp.where(
            low, dup_ref[send(2 * q)], dup_ref[send(2 * q + 1)]
        ).astype(bf16)


def emit_mirror(msg_ref, prod_ref, inv_ref, low):
    for q in range(PEERS):
        msg_ref[q, MC : 2 * MC, :] = jnp.where(
            low, prod_ref[inv_ref[2 * q]], prod_ref[inv_ref[2 * q + 1]]
        ).astype(bf16)


def invert_slots(inv_ref, src_ref):
    for i in range(RB):
        for k in (1, 2):
            inv_ref[src_ref[k, i] - RB] = 2 * i + k - 1


def mirror_products(dup_ref, wd_ref, prod_ref):
    for i in range(RB):
        prod = dot(dup_ref[i][:, 0:B].astype(bf16), wd_ref[i], NN)
        prod_ref[2 * i] = prod[:, 0:128]
        prod_ref[2 * i + 1] = prod[:, 128:256]


def starter(sems):
    taken = iter(range(sems.shape[0]))

    def start(source, target):
        copy = pltpu.make_async_copy(source, target, sems.at[next(taken)])
        copy.start()
        return copy

    return start


def unpack_rows(rows_ref, hb_ref):
    for j in range(32):
        rows_ref[STRIDE * j : STRIDE * j + 32, :] = hb_ref[:, 128 * j : 128 * (j + 1)].astype(f32)


def unpacked_row(rows_ref, i):
    return rows_ref[pl.ds(i, 32, stride=STRIDE), :]


def first_message_kernel(src_hbm, send_hbm, v_hbm, hb_hbm, msg_hbm, wd_hbm, table_hbm, keep_hbm, src_ref, send_ref, srcv_ref, sendv_ref, table_ref, v_ref, hb_ref, msg_ref, wd_ref, rows_ref, pair_ref, dup_ref, prod_ref, inv_ref, sems):
    low = low_half()
    start = starter(sems)
    blocks = [start(hb_hbm.at[k], hb_ref.at[k - 1]) for k in (1, 2)]
    vectors = start(v_hbm, v_ref)
    send = start(send_hbm, send_ref)
    src = start(src_hbm, src_ref)
    tables = [start(src_hbm, srcv_ref), start(send_hbm, sendv_ref)]
    vectors.wait()
    keep_out = start(v_ref, keep_hbm.at[0:MC, :])
    for t in range(RB // 2):
        tile = v_ref[:, 128 * t : 128 * (t + 1)].astype(f32)
        dup_ref[2 * t], dup_ref[2 * t + 1] = duplicate(tile, low)
    send.wait()
    emit_picks(msg_ref, dup_ref, lambda c: send_ref[0, c], low)
    picks_out = start(msg_ref.at[:, 0:MC, :], msg_hbm.at[:, 0:MC, :])
    for copy in tables:
        copy.wait()
    table_ref[...] = jnp.zeros(table_ref.shape, jnp.int32)
    table_ref[0:K, 0:RB] = srcv_ref[...]
    table_ref[K : K + 1, 0 : 2 * PEERS] = sendv_ref[...]
    table_out = start(table_ref, table_hbm.at[0:16, :])
    src.wait()
    invert_slots(inv_ref, src_ref)
    for k in (1, 2):
        blocks[k - 1].wait()
        unpack_rows(rows_ref.at[k - 1], hb_ref.at[k - 1])
        for i in range(RB):
            block = unpacked_row(rows_ref.at[k - 1], i)
            pair = pair_ref.at[k - 1, i]
            store_pair(pair, block, block, low)
            wd_ref[i, :, 128 * (k - 1) : 128 * k] = pair[...].astype(bf16)
    weights_out = start(wd_ref, wd_hbm.at[0:RB])
    mirror_products(dup_ref, wd_ref, prod_ref)
    emit_mirror(msg_ref, prod_ref, inv_ref, low)
    mirror_out = start(msg_ref.at[:, MC : 2 * MC, :], msg_hbm.at[:, MC : 2 * MC, :])
    for copy in (keep_out, table_out, picks_out, weights_out, mirror_out):
        copy.wait()


def local_sums(src_ref, v_ref, um_ref, um_ready, y_ref, dup_ref, dupb_ref, lhs_ref, mir_ref, *acc_refs):
    low = low_half()
    for t in range(RB // 2):
        tile = v_ref[:, 128 * t : 128 * (t + 1)].astype(f32)
        one, two = duplicate(tile, low)
        dup_ref[2 * t], dup_ref[2 * t + 1] = one, two
        dupb_ref[2 * t], dupb_ref[2 * t + 1] = one.astype(bf16), two.astype(bf16)

    def gather(i, _):
        for t, (k0, k1) in enumerate(LOCAL):
            j0 = i if k0 == 0 else jnp.minimum(src_ref[k0, i], RB - 1)
            j1 = jnp.minimum(src_ref[k1, i], RB - 1)
            lhs_ref[i, :, 128 * t : 128 * (t + 1)] = jnp.where(low, dup_ref[j0], dup_ref[j1]).astype(bf16)
        return 0

    lax.fori_loop(0, RB, gather, 0, unroll=8)
    um_ready()
    for i in range(RB):
        mir_ref[i] = dot(dupb_ref[i][:, 0:B], um_ref[i], NN)
    for i in range(RB):
        acc_refs[0][i, :, 0:B] = dot(lhs_ref[i], um_ref[i], NT)
    for acc_ref in acc_refs[1:]:
        acc_ref[...] = jnp.zeros(acc_ref.shape, f32)

    def scatter(i, _):
        for t, (k0, k1) in enumerate(LOCAL):
            j0 = i if k0 == 0 else jnp.minimum(src_ref[k0, i], RB - 1)
            j1 = jnp.minimum(src_ref[k1, i], RB - 1)
            part = mir_ref[i, :, 128 * t : 128 * (t + 1)]
            acc_refs[2 * (t % 2)][j0] += part
            acc_refs[2 * (t % 2) + 1][j1] += part
        return 0

    lax.fori_loop(0, RB, scatter, 0, unroll=8)
    for t in range(RB // 2):
        y_ref[:, 128 * t : 128 * (t + 1)] = folded(acc_refs[0], acc_refs[1], t, low) + folded(acc_refs[2], acc_refs[3], t, low)


def first_local_kernel(src_hbm, counts_hbm, v_hbm, hb_hbm, um_hbm, y_hbm, src_ref, counts_ref, v_ref, hb_ref, um_ref, y_ref, rows_ref, pair_ref, dup_ref, dupb_ref, lhs_ref, mir_ref, acc0_ref, acc1_ref, acc2_ref, acc3_ref, sems, hb_sems):
    low = low_half()
    start = starter(sems)
    counts = start(counts_hbm, counts_ref)

    def block_copies(t):
        k0, k1 = jnp.where(t == 0, 0, 2 * t + 2), 2 * t + 3
        return (
            pltpu.make_async_copy(hb_hbm.at[k0], hb_ref.at[2 * t], hb_sems.at[2 * t]),
            pltpu.make_async_copy(hb_hbm.at[k1], hb_ref.at[2 * t + 1], hb_sems.at[2 * t + 1]),
        )

    for t in range(len(LOCAL)):
        for copy in block_copies(t):
            copy.start()
    src = start(src_hbm, src_ref)
    vectors = start(v_hbm, v_ref)
    counts.wait()

    def relayout(t, _):
        for copy in block_copies(t):
            copy.wait()
        unpack_rows(rows_ref.at[0], hb_ref.at[2 * t])
        unpack_rows(rows_ref.at[1], hb_ref.at[2 * t + 1])
        k0, k1 = jnp.where(t == 0, 0, 2 * t + 2), 2 * t + 3
        lanes = pl.ds(pl.multiple_of(t * 128, 128), 128)
        for i in range(RB):
            count = counts_ref[i]
            one = jnp.where(k0 < count, unpacked_row(rows_ref.at[0], i), 0.0)
            two = jnp.where(k1 < count, unpacked_row(rows_ref.at[1], i), 0.0)
            store_pair(pair_ref.at[i], one, two, low)
            um_ref[i, :, lanes] = pair_ref[i].astype(bf16)
        return 0

    lax.fori_loop(0, len(LOCAL), relayout, 0)
    um_out = start(um_ref, um_hbm)
    src.wait()
    vectors.wait()
    local_sums(src_ref, v_ref, um_ref, lambda: None, y_ref, dup_ref, dupb_ref, lhs_ref, mir_ref, acc0_ref, acc1_ref, acc2_ref, acc3_ref)
    y_out = start(y_ref, y_hbm.at[0:MC, :])
    um_out.wait()
    y_out.wait()


def local_kernel(src_hbm, v_hbm, um_hbm, y_hbm, src_ref, v_ref, um_ref, y_ref, dup_ref, dupb_ref, lhs_ref, mir_ref, acc0_ref, acc1_ref, acc2_ref, acc3_ref, sems):
    start = starter(sems)
    vectors = start(v_hbm.at[0:MC, :], v_ref)
    src = start(src_hbm, src_ref)
    um = start(um_hbm, um_ref)
    vectors.wait()
    src.wait()
    local_sums(src_ref, v_ref, um_ref, um.wait, y_ref, dup_ref, dupb_ref, lhs_ref, mir_ref, acc0_ref, acc1_ref, acc2_ref, acc3_ref)
    start(y_ref, y_hbm.at[0:MC, :]).wait()


def remote_sum(table_ref, recv_ref, wd_ref, wd_ready, lhs_ref, low_ref, high_ref):
    lane = lax.broadcasted_iota(jnp.int32, (MC, 128), 1) // B

    def gather(i, _):
        for k in (1, 2):
            s = table_ref[k, i] - RB
            tile = recv_ref[s // 2, 0:MC, :].astype(f32)
            lhs_ref[i, :, 128 * (k - 1) : 128 * k] = jnp.where(lane == s % 2, tile, 0.0).astype(bf16)
        return 0

    lax.fori_loop(0, RB, gather, 0, unroll=8)
    wd_ready()
    for i in range(RB):
        low_ref[i, :, 0:B] = dot(lhs_ref[i], wd_ref[i], NT)
    high_ref[...] = jnp.zeros(high_ref.shape, f32)

    def scatter(q, _):
        tile = recv_ref[q, MC : 2 * MC, :].astype(f32)
        low_ref[table_ref[K, 2 * q]] += tile
        high_ref[table_ref[K, 2 * q + 1]] += tile
        return 0

    lax.fori_loop(0, PEERS, scatter, 0, unroll=8)


def folded(low_ref, high_ref, t, low):
    one, two = 2 * t, 2 * t + 1
    return jnp.where(
        low, low_ref[one] + pltpu.roll(high_ref[one], B, 1), pltpu.roll(low_ref[two], B, 1) + high_ref[two]
    )


def step_kernel(second, table_hbm, recv_ref, y_hbm, v_hbm, prev_hbm, wd_hbm, out_hbm, msg_hbm, table_ref, y_ref, v_ref, prev_ref, wd_ref, out_ref, msg_ref, lhs_ref, low_ref, high_ref, dup_ref, prod_ref, inv_ref, sems):
    low = low_half()
    start = starter(sems)
    table = start(table_hbm.at[0:16, :], table_ref)
    wd = start(wd_hbm.at[0:RB], wd_ref)
    terms = [start(y_hbm.at[0:MC, :], y_ref), start(v_hbm.at[0:MC, :], v_ref)]
    if second:
        terms.append(start(prev_hbm.at[0:MC, :], prev_ref))
    table.wait()
    invert_slots(inv_ref, table_ref)
    remote_sum(table_ref, recv_ref, wd_ref, wd.wait, lhs_ref, low_ref, high_ref)
    for copy in terms:
        copy.wait()
    for t in range(RB // 2):
        lanes = slice(128 * t, 128 * (t + 1))
        image = folded(low_ref, high_ref, t, low) + y_ref[:, lanes]
        if second:
            tile = 2.0 * (image - center_value * prev_ref[:, lanes].astype(f32)) / half_width - v_ref[:, lanes].astype(f32)
        else:
            tile = (image - center_value * v_ref[:, lanes].astype(f32)) / half_width
        tile = tile.astype(bf16)
        out_ref[:, lanes] = tile
        dup_ref[2 * t], dup_ref[2 * t + 1] = duplicate(tile.astype(f32), low)
    result_out = start(out_ref, out_hbm.at[0:MC, :])
    emit_picks(msg_ref, dup_ref, lambda c: table_ref[K, c], low)
    picks_out = start(msg_ref.at[:, 0:MC, :], msg_hbm.at[:, 0:MC, :])
    mirror_products(dup_ref, wd_ref, prod_ref)
    emit_mirror(msg_ref, prod_ref, inv_ref, low)
    mirror_out = start(msg_ref.at[:, MC : 2 * MC, :], msg_hbm.at[:, MC : 2 * MC, :])
    result_out.wait()
    picks_out.wait()
    mirror_out.wait()


def image_kernel(table_hbm, recv_ref, y_hbm, wd_hbm, *refs):
    own, other = refs[0:NY], refs[NY : 2 * NY]
    out_ref, table_ref, y_ref, wd_ref, lhs_ref, low_ref, high_ref, stack_ref, all_ref, sems = refs[2 * NY :]
    low = low_half()
    start = starter(sems)
    table = start(table_hbm.at[0:16, :], table_ref)
    wd = start(wd_hbm.at[0:RB], wd_ref)
    y_sum = start(y_hbm.at[0:MC, :], y_ref)
    y, c = lax.axis_index("y"), lax.axis_index("c")
    moves = [start(own[0], stack_ref.at[0:MC, :])]
    for d in range(NY):
        from_y = lax.rem(y + NY - d, NY) * NC
        for block, core in ((own[d], c), (other[d], 1 - c)):
            moves.append(start(block, all_ref.at[pl.ds(pl.multiple_of((from_y + core) * MC, MC), MC), :]))
    table.wait()
    remote_sum(table_ref, recv_ref, wd_ref, wd.wait, lhs_ref, low_ref, high_ref)
    y_sum.wait()
    for t in range(RB // 2):
        lanes = slice(128 * t, 128 * (t + 1))
        stack_ref[MC : 2 * MC, lanes] = (folded(low_ref, high_ref, t, low) + y_ref[:, lanes]).astype(bf16)
    for copy in moves:
        copy.wait()
    part = dot(stack_ref[...], all_ref[...], NT).astype(bf16)
    for z in range(NZ):
        out_ref[z] = part


def sum_z_kernel(in_ref, out_ref):
    total = in_ref[0].astype(f32)
    for z in range(1, NZ):
        total = total + in_ref[z].astype(f32)
    total = total.astype(bf16)
    for x in range(NX):
        out_ref[x] = total


def sum_x_kernel(in_ref, gram_ref, proj_ref):
    total = in_ref[0].astype(f32)
    for x in range(1, NX):
        total = total + in_ref[x].astype(f32)
    gram_ref[...] = total[0:MC, :]
    proj_ref[...] = total[MC : 2 * MC, :]


VM = pl.BlockSpec(memory_space=pltpu.VMEM)
ANY = pl.BlockSpec(memory_space=pl.ANY)
HBM = pl.BlockSpec(memory_space=pltpu.HBM)
shape = jax.ShapeDtypeStruct


def limit(mib):
    return pltpu.CompilerParams(vmem_limit_bytes=int(mib * MIB))


LOCAL_COST = pl.CostEstimate(flops=2 * 2 * RB * 10 * MC * B * B, bytes_accessed=20 * MIB, transcendentals=0)


def semaphores(count):
    return pltpu.SemaphoreType.DMA((count,))


def on_device(vectors, hblocks, counts, sources, send_rows):
    cols, width = vectors.shape
    row_axes, rows = ("z", "x"), hblocks.shape[0]
    msg_shape = shape((PEERS, 2 * MC, 128), bf16)
    um_shape = shape((rows, B, LW), bf16)
    vec = pltpu.VMEM((cols, width), bf16)
    vec_sum = pltpu.VMEM((cols, width), f32)
    msg = pltpu.VMEM(msg_shape.shape, bf16)
    wd_scratch = pltpu.VMEM((rows, B, 256), bf16)
    um_scratch = pltpu.VMEM(um_shape.shape, bf16)
    dup = pltpu.VMEM((rows, MC, 128), f32)
    dupb = pltpu.VMEM((rows, MC, 128), bf16)
    acc = pltpu.VMEM((rows, MC, 128), f32)
    prod = pltpu.VMEM((2 * rows, MC, 128), f32)
    inv = pltpu.SMEM((2 * PEERS,), jnp.int32)
    src = pltpu.SMEM((K, rows), jnp.int32)
    table_scratch = pltpu.SMEM((16, 128), jnp.int32)
    lhs = pltpu.VMEM((rows, MC, LW), bf16)
    lhs_remote = pltpu.VMEM((rows, MC, 256), bf16)
    mir = pltpu.VMEM((rows, MC, LW), f32)
    unpacked = pltpu.VMEM((2, STRIDE * 32, 128), f32)

    blocks = hblocks.transpose(1, 0, 2)
    sources = sources.T
    message, wd, table, kept = pl.pallas_call(
        first_message_kernel,
        out_shape=(
            msg_shape,
            shape((4 * rows, B, 256), bf16),
            shape((TABLE, 128), jnp.int32),
            shape((ROOM, width), bf16),
        ),
        in_specs=[HBM] * 4,
        out_specs=(HBM,) * 4,
        scratch_shapes=[
            src,
            pltpu.SMEM((1, 2 * PEERS), jnp.int32),
            pltpu.VMEM((K, rows), jnp.int32),
            pltpu.VMEM((1, 2 * PEERS), jnp.int32),
            pltpu.VMEM((16, 128), jnp.int32),
            vec,
            pltpu.VMEM((2, rows, B * B), bf16),
            msg,
            wd_scratch,
            unpacked,
            pltpu.VMEM((2, rows, B, 128), f32),
            dup,
            prod,
            inv,
            semaphores(12),
        ],
        compiler_params=limit(60),
        name="first_message",
    )(sources, send_rows[None], vectors, blocks)

    def exchange(message):
        return lax.all_to_all(message, row_axes, split_axis=0, concat_axis=0, tiled=True)

    received = exchange(message)
    local_scratch = [dup, dupb, lhs, mir, acc, acc, acc, acc]
    um, local = pl.pallas_call(
        first_local_kernel,
        out_shape=(um_shape, shape((ROOM, width), f32)),
        in_specs=[HBM] * 4,
        out_specs=(HBM, HBM),
        scratch_shapes=[
            src,
            pltpu.SMEM((rows,), jnp.int32),
            vec,
            pltpu.VMEM((2 * len(LOCAL), rows, B * B), bf16),
            um_scratch,
            vec_sum,
            unpacked,
            pltpu.VMEM((rows, B, 128), f32),
        ]
        + local_scratch
        + [semaphores(5), semaphores(2 * len(LOCAL))],
        compiler_params=limit(60),
        name="first_local",
    )(sources, counts, vectors, blocks)

    def local_part(block):
        return pl.pallas_call(
            local_kernel,
            out_shape=shape((ROOM, width), f32),
            in_specs=[HBM] * 3,
            out_specs=HBM,
            scratch_shapes=[src, vec, um_scratch, vec_sum] + local_scratch + [semaphores(4)],
            compiler_params=limit(60),
            cost_estimate=LOCAL_COST,
            name="local_product",
        )(sources, block, um)

    def next_step(second, received, local, previous):
        return pl.pallas_call(
            lambda *refs: step_kernel(second, *refs),
            out_shape=(shape((cols if second else ROOM, width), bf16), msg_shape),
            in_specs=[HBM, VM] + [HBM] * 4,
            out_specs=(HBM, HBM),
            scratch_shapes=[table_scratch, vec_sum, vec, vec, wd_scratch, vec, msg, lhs_remote, acc, acc, dup, prod, inv]
            + [semaphores(9)],
            compiler_params=limit(51.6),
            name="second_step" if second else "first_step",
        )(table, received, local, kept, previous, wd)

    first, message = next_step(False, received, local, kept)
    received = exchange(message)
    local = local_part(first)
    filtered, message = next_step(True, received, local, first)
    received = exchange(message)
    local = local_part(filtered)
    own = [filtered] + [
        lax.ppermute(filtered, "y", [(y, (y + d) % NY) for y in range(NY)]) for d in range(1, NY)
    ]
    local, *passed = lax.optimization_barrier((local, *own[1:]))
    own = own[:1] + passed
    other = [lax.ppermute(block, "c", [(0, 1), (1, 0)]) for block in own]
    part = pl.pallas_call(
        image_kernel,
        out_shape=shape((NZ, 2 * MC, NY * NC * MC), bf16),
        in_specs=[HBM, VM, HBM, HBM, HBM] + [ANY] * (2 * NY - 1),
        out_specs=VM,
        scratch_shapes=[
            table_scratch,
            vec_sum,
            wd_scratch,
            lhs_remote,
            acc,
            acc,
            pltpu.VMEM((2 * MC, width), bf16),
            pltpu.VMEM((NY * NC * MC, width), bf16),
            semaphores(5 + 2 * NY),
        ],
        compiler_params=limit(51.6),
        name="image",
    )(table, received, local, wd, *own, *other)
    part = lax.all_to_all(part, "z", split_axis=0, concat_axis=0, tiled=True)
    part = pl.pallas_call(
        sum_z_kernel,
        out_shape=shape((NX,) + part.shape[1:], bf16),
        compiler_params=limit(4),
        name="sum_z",
    )(part)
    part = lax.all_to_all(part, "x", split_axis=0, concat_axis=0, tiled=True)
    gram, projected = pl.pallas_call(
        sum_x_kernel,
        out_shape=(shape((MC, NY * NC * MC), f32),) * 2,
        compiler_params=limit(4),
        name="sum_x",
    )(part)
    return filtered, gram.T, projected.T


def solution(mesh):
    axes = Mesh(mesh.devices.reshape(NZ, NX, NY, NC), ("z", "x", "y", "c"))
    row, col = ("z", "x"), ("y", "c")
    return jax.shard_map(
        on_device,
        mesh=axes,
        in_specs=(P(col, row), P(row, None, None), P(row), P(row, None), P(row)),
        out_specs=(P(col, row), P(None, col), P(None, col)),
        check_vma=False,
    )
```

```python
import jax
import jax.numpy as jnp
from jax import lax
from jax.experimental import pallas as pl
from jax.experimental.pallas import tpu as pltpu
from jax.sharding import Mesh, PartitionSpec as P

B = 64
K = 12
RB = 32
MC = 32
PEERS = 32
NZ, NX, NY, NC = 8, 4, 4, 2
STRIDE = 40
ROOM = 1024
TABLE = 8192
LOCAL = ((0, 3), (4, 5), (6, 7), (8, 9), (10, 11))
LW = 128 * len(LOCAL)
center_value = 0.25
half_width = 1.5
bf16 = jnp.bfloat16
f32 = jnp.float32
MIB = 1024 * 1024

NN = (((1,), (0,)), ((), ()))
NT = (((1,), (1,)), ((), ()))


def low_half(rows=MC):
    return lax.broadcasted_iota(jnp.int32, (rows, 128), 1) < B


def dot(a, b, dims):
    return lax.dot_general(a, b, dims, preferred_element_type=f32)


def store_pair(even_odd_ref, first, second, low):
    even_odd_ref[pl.ds(0, 32, stride=2), :] = jnp.where(low, first, pltpu.roll(second, B, 1))
    even_odd_ref[pl.ds(1, 32, stride=2), :] = jnp.where(low, pltpu.roll(first, B, 1), second)


def duplicate(tile, low):
    turned = pltpu.roll(tile, B, 1)
    return jnp.where(low, tile, turned), jnp.where(low, turned, tile)


def emit_picks(msg_ref, dup_ref, send, low):
    for q in range(PEERS):
        msg_ref[q, 0:MC, :] = jnp.where(
            low, dup_ref[send(2 * q)], dup_ref[send(2 * q + 1)]
        ).astype(bf16)


def emit_mirror(msg_ref, prod_ref, inv_ref, low):
    for q in range(PEERS):
        msg_ref[q, MC : 2 * MC, :] = jnp.where(
            low, prod_ref[inv_ref[2 * q]], prod_ref[inv_ref[2 * q + 1]]
        ).astype(bf16)


def invert_slots(inv_ref, src_ref):
    for i in range(RB):
        for k in (1, 2):
            inv_ref[src_ref[k, i] - RB] = 2 * i + k - 1


def mirror_products(dup_ref, wd_ref, prod_ref):
    for i in range(RB):
        prod = dot(dup_ref[i][:, 0:B].astype(bf16), wd_ref[i], NN)
        prod_ref[2 * i] = prod[:, 0:128]
        prod_ref[2 * i + 1] = prod[:, 128:256]


def starter(sems):
    taken = iter(range(sems.shape[0]))

    def start(source, target):
        copy = pltpu.make_async_copy(source, target, sems.at[next(taken)])
        copy.start()
        return copy

    return start


def unpack_rows(rows_ref, hb_ref):
    for j in range(32):
        rows_ref[STRIDE * j : STRIDE * j + 32, :] = hb_ref[:, 128 * j : 128 * (j + 1)].astype(f32)


def unpacked_row(rows_ref, i):
    return rows_ref[pl.ds(i, 32, stride=STRIDE), :]


def first_message_kernel(src_hbm, send_hbm, v_hbm, hb_hbm, msg_hbm, wd_hbm, table_hbm, keep_hbm, src_ref, send_ref, srcv_ref, sendv_ref, table_ref, v_ref, hb_ref, msg_ref, wd_ref, rows_ref, pair_ref, dup_ref, prod_ref, inv_ref, sems):
    low = low_half()
    start = starter(sems)
    vectors = start(v_hbm, v_ref)
    send = start(send_hbm, send_ref)
    src = start(src_hbm, src_ref)
    blocks = [start(hb_hbm.at[k], hb_ref.at[k - 1]) for k in (1, 2)]
    tables = [start(src_hbm, srcv_ref), start(send_hbm, sendv_ref)]
    vectors.wait()
    for t in range(RB // 2):
        tile = v_ref[:, 128 * t : 128 * (t + 1)].astype(f32)
        dup_ref[2 * t], dup_ref[2 * t + 1] = duplicate(tile, low)
    send.wait()
    emit_picks(msg_ref, dup_ref, lambda c: send_ref[0, c], low)
    picks_out = start(msg_ref.at[:, 0:MC, :], msg_hbm.at[:, 0:MC, :])
    src.wait()
    invert_slots(inv_ref, src_ref)
    weights_out = []
    for k in (1, 2):
        blocks[k - 1].wait()
        unpack_rows(rows_ref.at[k - 1], hb_ref.at[k - 1])
        for i in range(RB):
            block = unpacked_row(rows_ref.at[k - 1], i)
            pair = pair_ref.at[k - 1, i]
            store_pair(pair, block, block, low)
            wd_ref[i, :, 128 * (k - 1) : 128 * k] = pair[...].astype(bf16)
        half = slice(128 * (k - 1), 128 * k)
        weights_out.append(start(wd_ref.at[:, :, half], wd_hbm.at[0:RB, :, half]))
    keep_out = start(v_ref, keep_hbm.at[0:MC, :])
    for copy in tables:
        copy.wait()
    table_ref[...] = jnp.zeros(table_ref.shape, jnp.int32)
    table_ref[0:K, 0:RB] = srcv_ref[...]
    table_ref[K : K + 1, 0 : 2 * PEERS] = sendv_ref[...]
    table_out = start(table_ref, table_hbm.at[0:16, :])
    mirror_products(dup_ref, wd_ref, prod_ref)
    emit_mirror(msg_ref, prod_ref, inv_ref, low)
    mirror_out = start(msg_ref.at[:, MC : 2 * MC, :], msg_hbm.at[:, MC : 2 * MC, :])
    for copy in (keep_out, table_out, picks_out, *weights_out, mirror_out):
        copy.wait()


def local_sums(src_ref, v_ref, um_ref, um_ready, y_ref, dup_ref, dupb_ref, lhs_ref, mir_ref, *acc_refs):
    low = low_half()
    for t in range(RB // 2):
        tile = v_ref[:, 128 * t : 128 * (t + 1)].astype(f32)
        one, two = duplicate(tile, low)
        dup_ref[2 * t], dup_ref[2 * t + 1] = one, two
        dupb_ref[2 * t], dupb_ref[2 * t + 1] = one.astype(bf16), two.astype(bf16)

    def gather(i, _):
        for t, (k0, k1) in enumerate(LOCAL):
            j0 = i if k0 == 0 else jnp.minimum(src_ref[k0, i], RB - 1)
            j1 = jnp.minimum(src_ref[k1, i], RB - 1)
            lhs_ref[i, :, 128 * t : 128 * (t + 1)] = jnp.where(low, dup_ref[j0], dup_ref[j1]).astype(bf16)
        return 0

    lax.fori_loop(0, RB, gather, 0, unroll=8)
    um_ready()
    for i in range(RB):
        mir_ref[i] = dot(dupb_ref[i][:, 0:B], um_ref[i], NN)
    for i in range(RB):
        acc_refs[0][i, :, 0:B] = dot(lhs_ref[i], um_ref[i], NT)
    for acc_ref in acc_refs[1:]:
        acc_ref[...] = jnp.zeros(acc_ref.shape, f32)

    def scatter(i, _):
        for t, (k0, k1) in enumerate(LOCAL):
            j0 = i if k0 == 0 else jnp.minimum(src_ref[k0, i], RB - 1)
            j1 = jnp.minimum(src_ref[k1, i], RB - 1)
            part = mir_ref[i, :, 128 * t : 128 * (t + 1)]
            acc_refs[2 * (t % 2)][j0] += part
            acc_refs[2 * (t % 2) + 1][j1] += part
        return 0

    lax.fori_loop(0, RB, scatter, 0, unroll=8)
    for t in range(RB // 2):
        y_ref[:, 128 * t : 128 * (t + 1)] = folded(acc_refs[0], acc_refs[1], t, low) + folded(acc_refs[2], acc_refs[3], t, low)


def first_local_kernel(src_hbm, counts_hbm, v_hbm, hb_hbm, um_hbm, y_hbm, src_ref, counts_ref, v_ref, hb_ref, um_ref, y_ref, rows_ref, pair_ref, dup_ref, dupb_ref, lhs_ref, mir_ref, acc0_ref, acc1_ref, acc2_ref, acc3_ref, sems, hb_sems):
    low = low_half()
    start = starter(sems)
    counts = start(counts_hbm, counts_ref)

    def block_copies(t):
        k0, k1 = jnp.where(t == 0, 0, 2 * t + 2), 2 * t + 3
        return (
            pltpu.make_async_copy(hb_hbm.at[k0], hb_ref.at[2 * t], hb_sems.at[2 * t]),
            pltpu.make_async_copy(hb_hbm.at[k1], hb_ref.at[2 * t + 1], hb_sems.at[2 * t + 1]),
        )

    for t in range(len(LOCAL)):
        for copy in block_copies(t):
            copy.start()
    src = start(src_hbm, src_ref)
    vectors = start(v_hbm, v_ref)
    counts.wait()

    def relayout(t, _):
        for copy in block_copies(t):
            copy.wait()
        unpack_rows(rows_ref.at[0], hb_ref.at[2 * t])
        unpack_rows(rows_ref.at[1], hb_ref.at[2 * t + 1])
        k0, k1 = jnp.where(t == 0, 0, 2 * t + 2), 2 * t + 3
        lanes = pl.ds(pl.multiple_of(t * 128, 128), 128)
        for i in range(RB):
            count = counts_ref[i]
            one = jnp.where(k0 < count, unpacked_row(rows_ref.at[0], i), 0.0)
            two = jnp.where(k1 < count, unpacked_row(rows_ref.at[1], i), 0.0)
            store_pair(pair_ref.at[i], one, two, low)
            um_ref[i, :, lanes] = pair_ref[i].astype(bf16)
        return 0

    lax.fori_loop(0, len(LOCAL), relayout, 0)
    um_out = start(um_ref, um_hbm)
    src.wait()
    vectors.wait()
    local_sums(src_ref, v_ref, um_ref, lambda: None, y_ref, dup_ref, dupb_ref, lhs_ref, mir_ref, acc0_ref, acc1_ref, acc2_ref, acc3_ref)
    y_out = start(y_ref, y_hbm.at[0:MC, :])
    um_out.wait()
    y_out.wait()


def local_kernel(src_hbm, v_hbm, um_hbm, y_hbm, src_ref, v_ref, um_ref, y_ref, dup_ref, dupb_ref, lhs_ref, mir_ref, acc0_ref, acc1_ref, acc2_ref, acc3_ref, sems):
    start = starter(sems)
    vectors = start(v_hbm.at[0:MC, :], v_ref)
    src = start(src_hbm, src_ref)
    um = start(um_hbm, um_ref)
    vectors.wait()
    src.wait()
    local_sums(src_ref, v_ref, um_ref, um.wait, y_ref, dup_ref, dupb_ref, lhs_ref, mir_ref, acc0_ref, acc1_ref, acc2_ref, acc3_ref)
    start(y_ref, y_hbm.at[0:MC, :]).wait()


def remote_sum(table_ref, recv_ref, wd_ref, wd_ready, lhs_ref, low_ref, high_ref):
    lane = lax.broadcasted_iota(jnp.int32, (MC, 128), 1) // B

    def gather(i, _):
        for k in (1, 2):
            s = table_ref[k, i] - RB
            tile = recv_ref[s // 2, 0:MC, :].astype(f32)
            lhs_ref[i, :, 128 * (k - 1) : 128 * k] = jnp.where(lane == s % 2, tile, 0.0).astype(bf16)
        return 0

    lax.fori_loop(0, RB, gather, 0, unroll=8)
    wd_ready()
    for i in range(RB):
        low_ref[i, :, 0:B] = dot(lhs_ref[i], wd_ref[i], NT)
    high_ref[...] = jnp.zeros(high_ref.shape, f32)

    def scatter(q, _):
        tile = recv_ref[q, MC : 2 * MC, :].astype(f32)
        low_ref[table_ref[K, 2 * q]] += tile
        high_ref[table_ref[K, 2 * q + 1]] += tile
        return 0

    lax.fori_loop(0, PEERS, scatter, 0, unroll=8)


def folded(low_ref, high_ref, t, low):
    one, two = 2 * t, 2 * t + 1
    return jnp.where(
        low, low_ref[one] + pltpu.roll(high_ref[one], B, 1), pltpu.roll(low_ref[two], B, 1) + high_ref[two]
    )


def step_kernel(second, table_hbm, recv_ref, y_hbm, v_hbm, prev_hbm, wd_hbm, out_hbm, msg_hbm, table_ref, y_ref, v_ref, prev_ref, wd_ref, out_ref, msg_ref, lhs_ref, low_ref, high_ref, dup_ref, prod_ref, inv_ref, sems):
    low = low_half()
    start = starter(sems)
    table = start(table_hbm.at[0:16, :], table_ref)
    wd = start(wd_hbm.at[0:RB], wd_ref)
    terms = [start(y_hbm.at[0:MC, :], y_ref), start(v_hbm.at[0:MC, :], v_ref)]
    if second:
        terms.append(start(prev_hbm.at[0:MC, :], prev_ref))
    table.wait()
    invert_slots(inv_ref, table_ref)
    remote_sum(table_ref, recv_ref, wd_ref, wd.wait, lhs_ref, low_ref, high_ref)
    for copy in terms:
        copy.wait()
    for t in range(RB // 2):
        lanes = slice(128 * t, 128 * (t + 1))
        image = folded(low_ref, high_ref, t, low) + y_ref[:, lanes]
        if second:
            tile = 2.0 * (image - center_value * prev_ref[:, lanes].astype(f32)) / half_width - v_ref[:, lanes].astype(f32)
        else:
            tile = (image - center_value * v_ref[:, lanes].astype(f32)) / half_width
        tile = tile.astype(bf16)
        out_ref[:, lanes] = tile
        dup_ref[2 * t], dup_ref[2 * t + 1] = duplicate(tile.astype(f32), low)
    result_out = start(out_ref, out_hbm.at[0:MC, :])
    emit_picks(msg_ref, dup_ref, lambda c: table_ref[K, c], low)
    picks_out = start(msg_ref.at[:, 0:MC, :], msg_hbm.at[:, 0:MC, :])
    mirror_products(dup_ref, wd_ref, prod_ref)
    emit_mirror(msg_ref, prod_ref, inv_ref, low)
    mirror_out = start(msg_ref.at[:, MC : 2 * MC, :], msg_hbm.at[:, MC : 2 * MC, :])
    result_out.wait()
    picks_out.wait()
    mirror_out.wait()


def image_kernel(table_hbm, recv_ref, y_hbm, wd_hbm, *refs):
    own, other = refs[0:NY], refs[NY : 2 * NY]
    out_ref, table_ref, y_ref, wd_ref, lhs_ref, low_ref, high_ref, stack_ref, all_ref, sems = refs[2 * NY :]
    low = low_half()
    start = starter(sems)
    table = start(table_hbm.at[0:16, :], table_ref)
    wd = start(wd_hbm.at[0:RB], wd_ref)
    y_sum = start(y_hbm.at[0:MC, :], y_ref)
    y, c = lax.axis_index("y"), lax.axis_index("c")
    moves = [start(own[0], stack_ref.at[0:MC, :])]
    for d in range(NY):
        from_y = lax.rem(y + NY - d, NY) * NC
        for block, core in ((own[d], c), (other[d], 1 - c)):
            moves.append(start(block, all_ref.at[pl.ds(pl.multiple_of((from_y + core) * MC, MC), MC), :]))
    table.wait()
    remote_sum(table_ref, recv_ref, wd_ref, wd.wait, lhs_ref, low_ref, high_ref)
    y_sum.wait()
    for t in range(RB // 2):
        lanes = slice(128 * t, 128 * (t + 1))
        stack_ref[MC : 2 * MC, lanes] = (folded(low_ref, high_ref, t, low) + y_ref[:, lanes]).astype(bf16)
    for copy in moves:
        copy.wait()
    part = dot(stack_ref[...], all_ref[...], NT).astype(bf16)
    for z in range(NZ):
        out_ref[z] = part


def sum_z_kernel(in_ref, out_ref):
    total = in_ref[0].astype(f32)
    for z in range(1, NZ):
        total = total + in_ref[z].astype(f32)
    total = total.astype(bf16)
    for x in range(NX):
        out_ref[x] = total


def sum_x_kernel(in_ref, gram_ref, proj_ref):
    total = in_ref[0].astype(f32)
    for x in range(1, NX):
        total = total + in_ref[x].astype(f32)
    gram_ref[...] = total[0:MC, :]
    proj_ref[...] = total[MC : 2 * MC, :]


VM = pl.BlockSpec(memory_space=pltpu.VMEM)
ANY = pl.BlockSpec(memory_space=pl.ANY)
HBM = pl.BlockSpec(memory_space=pltpu.HBM)
shape = jax.ShapeDtypeStruct


def limit(mib):
    return pltpu.CompilerParams(vmem_limit_bytes=int(mib * MIB))


LOCAL_COST = pl.CostEstimate(flops=2 * 2 * RB * 10 * MC * B * B, bytes_accessed=20 * MIB, transcendentals=0)


def semaphores(count):
    return pltpu.SemaphoreType.DMA((count,))


def on_device(vectors, hblocks, counts, sources, send_rows):
    cols, width = vectors.shape
    row_axes, rows = ("z", "x"), hblocks.shape[0]
    msg_shape = shape((PEERS, 2 * MC, 128), bf16)
    um_shape = shape((rows, B, LW), bf16)
    vec = pltpu.VMEM((cols, width), bf16)
    vec_sum = pltpu.VMEM((cols, width), f32)
    msg = pltpu.VMEM(msg_shape.shape, bf16)
    wd_scratch = pltpu.VMEM((rows, B, 256), bf16)
    um_scratch = pltpu.VMEM(um_shape.shape, bf16)
    dup = pltpu.VMEM((rows, MC, 128), f32)
    dupb = pltpu.VMEM((rows, MC, 128), bf16)
    acc = pltpu.VMEM((rows, MC, 128), f32)
    prod = pltpu.VMEM((2 * rows, MC, 128), f32)
    inv = pltpu.SMEM((2 * PEERS,), jnp.int32)
    src = pltpu.SMEM((K, rows), jnp.int32)
    table_scratch = pltpu.SMEM((16, 128), jnp.int32)
    lhs = pltpu.VMEM((rows, MC, LW), bf16)
    lhs_remote = pltpu.VMEM((rows, MC, 256), bf16)
    mir = pltpu.VMEM((rows, MC, LW), f32)
    unpacked = pltpu.VMEM((2, STRIDE * 32, 128), f32)

    blocks = hblocks.transpose(1, 0, 2)
    sources = sources.T
    message, wd, table, kept = pl.pallas_call(
        first_message_kernel,
        out_shape=(
            msg_shape,
            shape((4 * rows, B, 256), bf16),
            shape((TABLE, 128), jnp.int32),
            shape((ROOM, width), bf16),
        ),
        in_specs=[HBM] * 4,
        out_specs=(HBM,) * 4,
        scratch_shapes=[
            src,
            pltpu.SMEM((1, 2 * PEERS), jnp.int32),
            pltpu.VMEM((K, rows), jnp.int32),
            pltpu.VMEM((1, 2 * PEERS), jnp.int32),
            pltpu.VMEM((16, 128), jnp.int32),
            vec,
            pltpu.VMEM((2, rows, B * B), bf16),
            msg,
            wd_scratch,
            unpacked,
            pltpu.VMEM((2, rows, B, 128), f32),
            dup,
            prod,
            inv,
            semaphores(13),
        ],
        compiler_params=limit(60),
        name="first_message",
    )(sources, send_rows[None], vectors, blocks)

    def exchange(message):
        return lax.all_to_all(message, row_axes, split_axis=0, concat_axis=0, tiled=True)

    received = exchange(message)
    local_scratch = [dup, dupb, lhs, mir, acc, acc, acc, acc]
    um, local = pl.pallas_call(
        first_local_kernel,
        out_shape=(um_shape, shape((ROOM, width), f32)),
        in_specs=[HBM] * 4,
        out_specs=(HBM, HBM),
        scratch_shapes=[
            src,
            pltpu.SMEM((rows,), jnp.int32),
            vec,
            pltpu.VMEM((2 * len(LOCAL), rows, B * B), bf16),
            um_scratch,
            vec_sum,
            unpacked,
            pltpu.VMEM((rows, B, 128), f32),
        ]
        + local_scratch
        + [semaphores(5), semaphores(2 * len(LOCAL))],
        compiler_params=limit(60),
        name="first_local",
    )(sources, counts, vectors, blocks)

    def local_part(block):
        return pl.pallas_call(
            local_kernel,
            out_shape=shape((ROOM, width), f32),
            in_specs=[HBM] * 3,
            out_specs=HBM,
            scratch_shapes=[src, vec, um_scratch, vec_sum] + local_scratch + [semaphores(4)],
            compiler_params=limit(60),
            cost_estimate=LOCAL_COST,
            name="local_product",
        )(sources, block, um)

    def next_step(second, received, local, previous):
        return pl.pallas_call(
            lambda *refs: step_kernel(second, *refs),
            out_shape=(shape((cols if second else ROOM, width), bf16), msg_shape),
            in_specs=[HBM, VM] + [HBM] * 4,
            out_specs=(HBM, HBM),
            scratch_shapes=[table_scratch, vec_sum, vec, vec, wd_scratch, vec, msg, lhs_remote, acc, acc, dup, prod, inv]
            + [semaphores(9)],
            compiler_params=limit(51.6),
            name="second_step" if second else "first_step",
        )(table, received, local, kept, previous, wd)

    first, message = next_step(False, received, local, kept)
    received = exchange(message)
    local = local_part(first)
    filtered, message = next_step(True, received, local, first)
    received = exchange(message)
    local = local_part(filtered)
    own = [filtered] + [
        lax.ppermute(filtered, "y", [(y, (y + d) % NY) for y in range(NY)]) for d in range(1, NY)
    ]
    local, *passed = lax.optimization_barrier((local, *own[1:]))
    own = own[:1] + passed
    other = [lax.ppermute(block, "c", [(0, 1), (1, 0)]) for block in own]
    part = pl.pallas_call(
        image_kernel,
        out_shape=shape((NZ, 2 * MC, NY * NC * MC), bf16),
        in_specs=[HBM, VM, HBM, HBM, HBM] + [ANY] * (2 * NY - 1),
        out_specs=VM,
        scratch_shapes=[
            table_scratch,
            vec_sum,
            wd_scratch,
            lhs_remote,
            acc,
            acc,
            pltpu.VMEM((2 * MC, width), bf16),
            pltpu.VMEM((NY * NC * MC, width), bf16),
            semaphores(5 + 2 * NY),
        ],
        compiler_params=limit(51.6),
        name="image",
    )(table, received, local, wd, *own, *other)
    part = lax.all_to_all(part, "z", split_axis=0, concat_axis=0, tiled=True)
    part = pl.pallas_call(
        sum_z_kernel,
        out_shape=shape((NX,) + part.shape[1:], bf16),
        compiler_params=limit(4),
        name="sum_z",
    )(part)
    part = lax.all_to_all(part, "x", split_axis=0, concat_axis=0, tiled=True)
    gram, projected = pl.pallas_call(
        sum_x_kernel,
        out_shape=(shape((MC, NY * NC * MC), f32),) * 2,
        compiler_params=limit(4),
        name="sum_x",
    )(part)
    return filtered, gram.T, projected.T


def solution(mesh):
    axes = Mesh(mesh.devices.reshape(NZ, NX, NY, NC), ("z", "x", "y", "c"))
    row, col = ("z", "x"), ("y", "c")
    return jax.shard_map(
        on_device,
        mesh=axes,
        in_specs=(P(col, row), P(row, None, None), P(row), P(row, None), P(row)),
        out_specs=(P(col, row), P(None, col), P(None, col)),
        check_vma=False,
    )
```

```python
import jax
import jax.numpy as jnp
from jax import lax
from jax.experimental import pallas as pl
from jax.experimental.pallas import tpu as pltpu
from jax.sharding import Mesh, PartitionSpec as P

B = 64
K = 12
RB = 32
MC = 32
PEERS = 32
NZ, NX, NY, NC = 8, 4, 4, 2
STRIDE = 40
ROOM = 1024
TABLE = 8192
LOCAL = ((0, 3), (4, 5), (6, 7), (8, 9), (10, 11))
LW = 128 * len(LOCAL)
center_value = 0.25
half_width = 1.5
bf16 = jnp.bfloat16
f32 = jnp.float32
MIB = 1024 * 1024

NN = (((1,), (0,)), ((), ()))
NT = (((1,), (1,)), ((), ()))


def low_half(rows=MC):
    return lax.broadcasted_iota(jnp.int32, (rows, 128), 1) < B


def dot(a, b, dims):
    return lax.dot_general(a, b, dims, preferred_element_type=f32)


def store_pair(even_odd_ref, first, second, low):
    even_odd_ref[pl.ds(0, 32, stride=2), :] = jnp.where(low, first, pltpu.roll(second, B, 1))
    even_odd_ref[pl.ds(1, 32, stride=2), :] = jnp.where(low, pltpu.roll(first, B, 1), second)


def duplicate(tile, low):
    turned = pltpu.roll(tile, B, 1)
    return jnp.where(low, tile, turned), jnp.where(low, turned, tile)


def emit_picks(msg_ref, dup_ref, send, low):
    for q in range(PEERS):
        msg_ref[q, 0:MC, :] = jnp.where(
            low, dup_ref[send(2 * q)], dup_ref[send(2 * q + 1)]
        ).astype(bf16)


def emit_mirror(msg_ref, prod_ref, inv_ref, low):
    for q in range(PEERS):
        msg_ref[q, MC : 2 * MC, :] = jnp.where(
            low, prod_ref[inv_ref[2 * q]], prod_ref[inv_ref[2 * q + 1]]
        ).astype(bf16)


def invert_slots(inv_ref, src_ref):
    for i in range(RB):
        for k in (1, 2):
            inv_ref[src_ref[k, i] - RB] = 2 * i + k - 1


def mirror_products(dup_ref, wd_ref, prod_ref):
    for i in range(RB):
        prod = dot(dup_ref[i][:, 0:B].astype(bf16), wd_ref[i], NN)
        prod_ref[2 * i] = prod[:, 0:128]
        prod_ref[2 * i + 1] = prod[:, 128:256]


def starter(sems):
    taken = iter(range(sems.shape[0]))

    def start(source, target):
        copy = pltpu.make_async_copy(source, target, sems.at[next(taken)])
        copy.start()
        return copy

    return start


def unpack_rows(rows_ref, hb_ref):
    for j in range(32):
        rows_ref[STRIDE * j : STRIDE * j + 32, :] = hb_ref[:, 128 * j : 128 * (j + 1)].astype(f32)


def unpacked_row(rows_ref, i):
    return rows_ref[pl.ds(i, 32, stride=STRIDE), :]


def first_message_kernel(src_hbm, send_hbm, v_hbm, hb_hbm, msg_hbm, wd_hbm, table_hbm, keep_hbm, src_ref, send_ref, srcv_ref, sendv_ref, table_ref, v_ref, hb_ref, msg_ref, wd_ref, rows_ref, pair_ref, dup_ref, prod_ref, inv_ref, sems):
    low = low_half()
    start = starter(sems)
    vectors = start(v_hbm, v_ref)
    send = start(send_hbm, send_ref)
    src = start(src_hbm, src_ref)
    blocks = [start(hb_hbm.at[k], hb_ref.at[k - 1]) for k in (1, 2)]
    tables = [start(src_hbm, srcv_ref), start(send_hbm, sendv_ref)]
    vectors.wait()
    for t in range(RB // 2):
        tile = v_ref[:, 128 * t : 128 * (t + 1)].astype(f32)
        dup_ref[2 * t], dup_ref[2 * t + 1] = duplicate(tile, low)
    send.wait()
    emit_picks(msg_ref, dup_ref, lambda c: send_ref[0, c], low)
    picks_out = start(msg_ref.at[:, 0:MC, :], msg_hbm.at[:, 0:MC, :])
    src.wait()
    invert_slots(inv_ref, src_ref)
    weights_out = []
    for k in (1, 2):
        blocks[k - 1].wait()
        unpack_rows(rows_ref.at[k - 1], hb_ref.at[k - 1])
        for i in range(RB):
            block = unpacked_row(rows_ref.at[k - 1], i)
            pair = pair_ref.at[k - 1, i]
            store_pair(pair, block, block, low)
            wd_ref[i, :, 128 * (k - 1) : 128 * k] = pair[...].astype(bf16)
        half = slice(128 * (k - 1), 128 * k)
        weights_out.append(start(wd_ref.at[:, :, half], wd_hbm.at[0:RB, :, half]))
    keep_out = start(v_ref, keep_hbm.at[0:MC, :])
    for copy in tables:
        copy.wait()
    table_ref[...] = jnp.zeros(table_ref.shape, jnp.int32)
    table_ref[0:K, 0:RB] = srcv_ref[...]
    table_ref[K : K + 1, 0 : 2 * PEERS] = sendv_ref[...]
    table_out = start(table_ref, table_hbm.at[0:16, :])
    mirror_products(dup_ref, wd_ref, prod_ref)
    emit_mirror(msg_ref, prod_ref, inv_ref, low)
    mirror_out = start(msg_ref.at[:, MC : 2 * MC, :], msg_hbm.at[:, MC : 2 * MC, :])
    for copy in (keep_out, table_out, picks_out, *weights_out, mirror_out):
        copy.wait()


def local_sums(src_ref, v_ref, um_ref, um_ready, y_ref, dup_ref, dupb_ref, lhs_ref, mir_ref, *acc_refs):
    low = low_half()
    for t in range(RB // 2):
        tile = v_ref[:, 128 * t : 128 * (t + 1)].astype(f32)
        one, two = duplicate(tile, low)
        dup_ref[2 * t], dup_ref[2 * t + 1] = one, two
        dupb_ref[2 * t], dupb_ref[2 * t + 1] = one.astype(bf16), two.astype(bf16)

    def gather(i, _):
        for t, (k0, k1) in enumerate(LOCAL):
            j0 = i if k0 == 0 else jnp.minimum(src_ref[k0, i], RB - 1)
            j1 = jnp.minimum(src_ref[k1, i], RB - 1)
            lhs_ref[i, :, 128 * t : 128 * (t + 1)] = jnp.where(low, dup_ref[j0], dup_ref[j1]).astype(bf16)
        return 0

    lax.fori_loop(0, RB, gather, 0, unroll=8)
    um_ready()
    for i in range(RB):
        mir_ref[i] = dot(dupb_ref[i][:, 0:B], um_ref[i], NN)
    for i in range(RB):
        acc_refs[0][i, :, 0:B] = dot(lhs_ref[i], um_ref[i], NT)
    for acc_ref in acc_refs[1:]:
        acc_ref[...] = jnp.zeros(acc_ref.shape, f32)

    def scatter(i, _):
        for t, (k0, k1) in enumerate(LOCAL):
            j0 = i if k0 == 0 else jnp.minimum(src_ref[k0, i], RB - 1)
            j1 = jnp.minimum(src_ref[k1, i], RB - 1)
            part = mir_ref[i, :, 128 * t : 128 * (t + 1)]
            acc_refs[2 * (t % 2)][j0] += part
            acc_refs[2 * (t % 2) + 1][j1] += part
        return 0

    lax.fori_loop(0, RB, scatter, 0, unroll=8)
    for t in range(RB // 2):
        y_ref[:, 128 * t : 128 * (t + 1)] = folded(acc_refs[0], acc_refs[1], t, low) + folded(acc_refs[2], acc_refs[3], t, low)


def first_local_kernel(src_hbm, counts_hbm, v_hbm, hb_hbm, um_hbm, y_hbm, src_ref, counts_ref, v_ref, hb_ref, um_ref, y_ref, rows_ref, pair_ref, dup_ref, dupb_ref, lhs_ref, mir_ref, acc0_ref, acc1_ref, acc2_ref, acc3_ref, sems, hb_sems):
    low = low_half()
    start = starter(sems)
    counts = start(counts_hbm, counts_ref)

    def block_copies(t):
        k0, k1 = jnp.where(t == 0, 0, 2 * t + 2), 2 * t + 3
        return (
            pltpu.make_async_copy(hb_hbm.at[k0], hb_ref.at[2 * t], hb_sems.at[2 * t]),
            pltpu.make_async_copy(hb_hbm.at[k1], hb_ref.at[2 * t + 1], hb_sems.at[2 * t + 1]),
        )

    for t in range(len(LOCAL)):
        for copy in block_copies(t):
            copy.start()
    src = start(src_hbm, src_ref)
    vectors = start(v_hbm, v_ref)
    counts.wait()

    def relayout(t, _):
        for copy in block_copies(t):
            copy.wait()
        unpack_rows(rows_ref.at[0], hb_ref.at[2 * t])
        unpack_rows(rows_ref.at[1], hb_ref.at[2 * t + 1])
        k0, k1 = jnp.where(t == 0, 0, 2 * t + 2), 2 * t + 3
        lanes = pl.ds(pl.multiple_of(t * 128, 128), 128)
        for i in range(RB):
            count = counts_ref[i]
            one = jnp.where(k0 < count, unpacked_row(rows_ref.at[0], i), 0.0)
            two = jnp.where(k1 < count, unpacked_row(rows_ref.at[1], i), 0.0)
            store_pair(pair_ref.at[i], one, two, low)
            um_ref[i, :, lanes] = pair_ref[i].astype(bf16)
        return 0

    lax.fori_loop(0, len(LOCAL), relayout, 0)
    um_out = start(um_ref, um_hbm)
    src.wait()
    vectors.wait()
    local_sums(src_ref, v_ref, um_ref, lambda: None, y_ref, dup_ref, dupb_ref, lhs_ref, mir_ref, acc0_ref, acc1_ref, acc2_ref, acc3_ref)
    y_out = start(y_ref, y_hbm.at[0:MC, :])
    um_out.wait()
    y_out.wait()


def local_kernel(src_hbm, v_hbm, um_hbm, y_hbm, src_ref, v_ref, um_ref, y_ref, dup_ref, dupb_ref, lhs_ref, mir_ref, acc0_ref, acc1_ref, acc2_ref, acc3_ref, sems):
    start = starter(sems)
    vectors = start(v_hbm.at[0:MC, :], v_ref)
    src = start(src_hbm, src_ref)
    um = start(um_hbm, um_ref)
    vectors.wait()
    src.wait()
    local_sums(src_ref, v_ref, um_ref, um.wait, y_ref, dup_ref, dupb_ref, lhs_ref, mir_ref, acc0_ref, acc1_ref, acc2_ref, acc3_ref)
    start(y_ref, y_hbm.at[0:MC, :]).wait()


def remote_sum(table_ref, recv_ref, wd_ref, wd_ready, lhs_ref, low_ref, high_ref):
    lane = lax.broadcasted_iota(jnp.int32, (MC, 128), 1) // B

    def gather(i, _):
        for k in (1, 2):
            s = table_ref[k, i] - RB
            tile = recv_ref[s // 2, 0:MC, :].astype(f32)
            lhs_ref[i, :, 128 * (k - 1) : 128 * k] = jnp.where(lane == s % 2, tile, 0.0).astype(bf16)
        return 0

    lax.fori_loop(0, RB, gather, 0, unroll=8)
    wd_ready()
    for i in range(RB):
        low_ref[i, :, 0:B] = dot(lhs_ref[i], wd_ref[i], NT)
    high_ref[...] = jnp.zeros(high_ref.shape, f32)

    def scatter(q, _):
        tile = recv_ref[q, MC : 2 * MC, :].astype(f32)
        low_ref[table_ref[K, 2 * q]] += tile
        high_ref[table_ref[K, 2 * q + 1]] += tile
        return 0

    lax.fori_loop(0, PEERS, scatter, 0, unroll=8)


def folded(low_ref, high_ref, t, low):
    one, two = 2 * t, 2 * t + 1
    return jnp.where(
        low, low_ref[one] + pltpu.roll(high_ref[one], B, 1), pltpu.roll(low_ref[two], B, 1) + high_ref[two]
    )


def step_kernel(second, table_hbm, recv_ref, y_hbm, v_hbm, prev_hbm, wd_hbm, out_hbm, msg_hbm, table_ref, y_ref, v_ref, prev_ref, wd_ref, out_ref, msg_ref, lhs_ref, low_ref, high_ref, dup_ref, prod_ref, inv_ref, sems):
    low = low_half()
    start = starter(sems)
    table = start(table_hbm.at[0:16, :], table_ref)
    wd = start(wd_hbm.at[0:RB], wd_ref)
    terms = [start(y_hbm.at[0:MC, :], y_ref), start(v_hbm.at[0:MC, :], v_ref)]
    if second:
        terms.append(start(prev_hbm.at[0:MC, :], prev_ref))
    table.wait()
    invert_slots(inv_ref, table_ref)
    remote_sum(table_ref, recv_ref, wd_ref, wd.wait, lhs_ref, low_ref, high_ref)
    for copy in terms:
        copy.wait()
    for t in range(RB // 2):
        lanes = slice(128 * t, 128 * (t + 1))
        image = folded(low_ref, high_ref, t, low) + y_ref[:, lanes]
        if second:
            tile = 2.0 * (image - center_value * prev_ref[:, lanes].astype(f32)) / half_width - v_ref[:, lanes].astype(f32)
        else:
            tile = (image - center_value * v_ref[:, lanes].astype(f32)) / half_width
        tile = tile.astype(bf16)
        out_ref[:, lanes] = tile
        dup_ref[2 * t], dup_ref[2 * t + 1] = duplicate(tile.astype(f32), low)
    result_out = start(out_ref, out_hbm.at[0:MC, :])
    emit_picks(msg_ref, dup_ref, lambda c: table_ref[K, c], low)
    picks_out = start(msg_ref.at[:, 0:MC, :], msg_hbm.at[:, 0:MC, :])
    mirror_products(dup_ref, wd_ref, prod_ref)
    emit_mirror(msg_ref, prod_ref, inv_ref, low)
    mirror_out = start(msg_ref.at[:, MC : 2 * MC, :], msg_hbm.at[:, MC : 2 * MC, :])
    result_out.wait()
    picks_out.wait()
    mirror_out.wait()


def image_kernel(table_hbm, recv_ref, y_hbm, wd_hbm, *refs):
    own, other = refs[0:NY], refs[NY : 2 * NY]
    out_ref, table_ref, y_ref, wd_ref, lhs_ref, low_ref, high_ref, stack_ref, all_ref, sems = refs[2 * NY :]
    low = low_half()
    start = starter(sems)
    table = start(table_hbm.at[0:16, :], table_ref)
    wd = start(wd_hbm.at[0:RB], wd_ref)
    y_sum = start(y_hbm.at[0:MC, :], y_ref)
    y, c = lax.axis_index("y"), lax.axis_index("c")
    moves = [start(own[0], stack_ref.at[0:MC, :])]
    for d in range(NY):
        from_y = lax.rem(y + NY - d, NY) * NC
        for block, core in ((own[d], c), (other[d], 1 - c)):
            moves.append(start(block, all_ref.at[pl.ds(pl.multiple_of((from_y + core) * MC, MC), MC), :]))
    table.wait()
    remote_sum(table_ref, recv_ref, wd_ref, wd.wait, lhs_ref, low_ref, high_ref)
    y_sum.wait()
    for t in range(RB // 2):
        lanes = slice(128 * t, 128 * (t + 1))
        stack_ref[MC : 2 * MC, lanes] = (folded(low_ref, high_ref, t, low) + y_ref[:, lanes]).astype(bf16)
    for copy in moves:
        copy.wait()
    part = dot(stack_ref[...], all_ref[...], NT).astype(bf16)
    for x in range(NX):
        out_ref[x] = part


def sum_x_kernel(in_ref, out_ref):
    total = in_ref[0].astype(f32)
    for x in range(1, NX):
        total = total + in_ref[x].astype(f32)
    total = total.astype(bf16)
    for z in range(NZ):
        out_ref[z] = total


def sum_z_kernel(in_ref, gram_ref, proj_ref):
    total = in_ref[0].astype(f32)
    for z in range(1, NZ):
        total = total + in_ref[z].astype(f32)
    gram_ref[...] = total[0:MC, :]
    proj_ref[...] = total[MC : 2 * MC, :]


VM = pl.BlockSpec(memory_space=pltpu.VMEM)
ANY = pl.BlockSpec(memory_space=pl.ANY)
HBM = pl.BlockSpec(memory_space=pltpu.HBM)
shape = jax.ShapeDtypeStruct


def limit(mib):
    return pltpu.CompilerParams(vmem_limit_bytes=int(mib * MIB))


LOCAL_COST = pl.CostEstimate(flops=2 * 2 * RB * 10 * MC * B * B, bytes_accessed=20 * MIB, transcendentals=0)


def semaphores(count):
    return pltpu.SemaphoreType.DMA((count,))


def on_device(vectors, hblocks, counts, sources, send_rows):
    cols, width = vectors.shape
    row_axes, rows = ("z", "x"), hblocks.shape[0]
    msg_shape = shape((PEERS, 2 * MC, 128), bf16)
    um_shape = shape((rows, B, LW), bf16)
    vec = pltpu.VMEM((cols, width), bf16)
    vec_sum = pltpu.VMEM((cols, width), f32)
    msg = pltpu.VMEM(msg_shape.shape, bf16)
    wd_scratch = pltpu.VMEM((rows, B, 256), bf16)
    um_scratch = pltpu.VMEM(um_shape.shape, bf16)
    dup = pltpu.VMEM((rows, MC, 128), f32)
    dupb = pltpu.VMEM((rows, MC, 128), bf16)
    acc = pltpu.VMEM((rows, MC, 128), f32)
    prod = pltpu.VMEM((2 * rows, MC, 128), f32)
    inv = pltpu.SMEM((2 * PEERS,), jnp.int32)
    src = pltpu.SMEM((K, rows), jnp.int32)
    table_scratch = pltpu.SMEM((16, 128), jnp.int32)
    lhs = pltpu.VMEM((rows, MC, LW), bf16)
    lhs_remote = pltpu.VMEM((rows, MC, 256), bf16)
    mir = pltpu.VMEM((rows, MC, LW), f32)
    unpacked = pltpu.VMEM((2, STRIDE * 32, 128), f32)

    blocks = hblocks.transpose(1, 0, 2)
    sources = sources.T
    message, wd, table, kept = pl.pallas_call(
        first_message_kernel,
        out_shape=(
            msg_shape,
            shape((4 * rows, B, 256), bf16),
            shape((TABLE, 128), jnp.int32),
            shape((ROOM, width), bf16),
        ),
        in_specs=[HBM] * 4,
        out_specs=(HBM,) * 4,
        scratch_shapes=[
            src,
            pltpu.SMEM((1, 2 * PEERS), jnp.int32),
            pltpu.VMEM((K, rows), jnp.int32),
            pltpu.VMEM((1, 2 * PEERS), jnp.int32),
            pltpu.VMEM((16, 128), jnp.int32),
            vec,
            pltpu.VMEM((2, rows, B * B), bf16),
            msg,
            wd_scratch,
            unpacked,
            pltpu.VMEM((2, rows, B, 128), f32),
            dup,
            prod,
            inv,
            semaphores(13),
        ],
        compiler_params=limit(60),
        name="first_message",
    )(sources, send_rows[None], vectors, blocks)

    def exchange(message):
        return lax.all_to_all(message, row_axes, split_axis=0, concat_axis=0, tiled=True)

    received = exchange(message)
    local_scratch = [dup, dupb, lhs, mir, acc, acc, acc, acc]
    um, local = pl.pallas_call(
        first_local_kernel,
        out_shape=(um_shape, shape((ROOM, width), f32)),
        in_specs=[HBM] * 4,
        out_specs=(HBM, HBM),
        scratch_shapes=[
            src,
            pltpu.SMEM((rows,), jnp.int32),
            vec,
            pltpu.VMEM((2 * len(LOCAL), rows, B * B), bf16),
            um_scratch,
            vec_sum,
            unpacked,
            pltpu.VMEM((rows, B, 128), f32),
        ]
        + local_scratch
        + [semaphores(5), semaphores(2 * len(LOCAL))],
        compiler_params=limit(60),
        name="first_local",
    )(sources, counts, vectors, blocks)

    def local_part(block):
        return pl.pallas_call(
            local_kernel,
            out_shape=shape((ROOM, width), f32),
            in_specs=[HBM] * 3,
            out_specs=HBM,
            scratch_shapes=[src, vec, um_scratch, vec_sum] + local_scratch + [semaphores(4)],
            compiler_params=limit(60),
            cost_estimate=LOCAL_COST,
            name="local_product",
        )(sources, block, um)

    def next_step(second, received, local, previous):
        return pl.pallas_call(
            lambda *refs: step_kernel(second, *refs),
            out_shape=(shape((cols if second else ROOM, width), bf16), msg_shape),
            in_specs=[HBM, VM] + [HBM] * 4,
            out_specs=(HBM, HBM),
            scratch_shapes=[table_scratch, vec_sum, vec, vec, wd_scratch, vec, msg, lhs_remote, acc, acc, dup, prod, inv]
            + [semaphores(9)],
            compiler_params=limit(51.6),
            name="second_step" if second else "first_step",
        )(table, received, local, kept, previous, wd)

    first, message = next_step(False, received, local, kept)
    received = exchange(message)
    local = local_part(first)
    filtered, message = next_step(True, received, local, first)
    received = exchange(message)
    local = local_part(filtered)
    own = [filtered] + [
        lax.ppermute(filtered, "y", [(y, (y + d) % NY) for y in range(NY)]) for d in range(1, NY)
    ]
    local, *passed = lax.optimization_barrier((local, *own[1:]))
    own = own[:1] + passed
    other = [lax.ppermute(block, "c", [(0, 1), (1, 0)]) for block in own]
    part = pl.pallas_call(
        image_kernel,
        out_shape=shape((NX, 2 * MC, NY * NC * MC), bf16),
        in_specs=[HBM, VM, HBM, HBM, HBM] + [ANY] * (2 * NY - 1),
        out_specs=VM,
        scratch_shapes=[
            table_scratch,
            vec_sum,
            wd_scratch,
            lhs_remote,
            acc,
            acc,
            pltpu.VMEM((2 * MC, width), bf16),
            pltpu.VMEM((NY * NC * MC, width), bf16),
            semaphores(5 + 2 * NY),
        ],
        compiler_params=limit(51.6),
        name="image",
    )(table, received, local, wd, *own, *other)
    part = lax.all_to_all(part, "x", split_axis=0, concat_axis=0, tiled=True)
    part = pl.pallas_call(
        sum_x_kernel,
        out_shape=shape((NZ,) + part.shape[1:], bf16),
        compiler_params=limit(4),
        name="sum_x",
    )(part)
    part = lax.all_to_all(part, "z", split_axis=0, concat_axis=0, tiled=True)
    gram, projected = pl.pallas_call(
        sum_z_kernel,
        out_shape=(shape((MC, NY * NC * MC), f32),) * 2,
        compiler_params=limit(4),
        name="sum_z",
    )(part)
    return filtered, gram.T, projected.T


def solution(mesh):
    axes = Mesh(mesh.devices.reshape(NZ, NX, NY, NC), ("z", "x", "y", "c"))
    row, col = ("z", "x"), ("y", "c")
    return jax.shard_map(
        on_device,
        mesh=axes,
        in_specs=(P(col, row), P(row, None, None), P(row), P(row, None), P(row)),
        out_specs=(P(col, row), P(None, col), P(None, col)),
        check_vma=False,
    )
```

```python
import jax
import jax.numpy as jnp
from jax import lax
from jax.experimental import pallas as pl
from jax.experimental.pallas import tpu as pltpu
from jax.sharding import Mesh, PartitionSpec as P

B = 64
K = 12
RB = 32
MC = 32
PEERS = 32
NZ, NX, NY, NC = 8, 4, 4, 2
STRIDE = 40
SHIFTS = (0, 1, 3, 2)
ROOM = 1024
TABLE = 8192
LOCAL = ((0, 3), (4, 5), (6, 7), (8, 9), (10, 11))
LW = 128 * len(LOCAL)
center_value = 0.25
half_width = 1.5
bf16 = jnp.bfloat16
f32 = jnp.float32
MIB = 1024 * 1024

NN = (((1,), (0,)), ((), ()))
NT = (((1,), (1,)), ((), ()))


def low_half(rows=MC):
    return lax.broadcasted_iota(jnp.int32, (rows, 128), 1) < B


def dot(a, b, dims):
    return lax.dot_general(a, b, dims, preferred_element_type=f32)


def store_pair(even_odd_ref, first, second, low):
    even_odd_ref[pl.ds(0, 32, stride=2), :] = jnp.where(low, first, pltpu.roll(second, B, 1))
    even_odd_ref[pl.ds(1, 32, stride=2), :] = jnp.where(low, pltpu.roll(first, B, 1), second)


def duplicate(tile, low):
    turned = pltpu.roll(tile, B, 1)
    return jnp.where(low, tile, turned), jnp.where(low, turned, tile)


def emit_picks(msg_ref, dup_ref, send, low):
    for q in range(PEERS):
        msg_ref[q, 0:MC, :] = jnp.where(
            low, dup_ref[send(2 * q)], dup_ref[send(2 * q + 1)]
        ).astype(bf16)


def emit_mirror(msg_ref, prod_ref, inv_ref, low):
    for q in range(PEERS):
        msg_ref[q, MC : 2 * MC, :] = jnp.where(
            low, prod_ref[inv_ref[2 * q]], prod_ref[inv_ref[2 * q + 1]]
        ).astype(bf16)


def invert_slots(inv_ref, src_ref):
    for i in range(RB):
        for k in (1, 2):
            inv_ref[src_ref[k, i] - RB] = 2 * i + k - 1


def mirror_products(dup_ref, wd_ref, prod_ref):
    for i in range(RB):
        prod = dot(dup_ref[i][:, 0:B].astype(bf16), wd_ref[i], NN)
        prod_ref[2 * i] = prod[:, 0:128]
        prod_ref[2 * i + 1] = prod[:, 128:256]


def starter(sems):
    taken = iter(range(sems.shape[0]))

    def start(source, target):
        copy = pltpu.make_async_copy(source, target, sems.at[next(taken)])
        copy.start()
        return copy

    return start


def unpack_rows(rows_ref, hb_ref):
    for j in range(32):
        rows_ref[STRIDE * j : STRIDE * j + 32, :] = hb_ref[:, 128 * j : 128 * (j + 1)].astype(f32)


def unpacked_row(rows_ref, i):
    return rows_ref[pl.ds(i, 32, stride=STRIDE), :]


def first_message_kernel(src_hbm, send_hbm, v_hbm, hb_hbm, msg_hbm, wd_hbm, table_hbm, keep_hbm, src_ref, send_ref, srcv_ref, sendv_ref, table_ref, v_ref, hb_ref, msg_ref, wd_ref, rows_ref, pair_ref, dup_ref, prod_ref, inv_ref, sems):
    low = low_half()
    start = starter(sems)
    vectors = start(v_hbm, v_ref)
    send = start(send_hbm, send_ref)
    src = start(src_hbm, src_ref)
    blocks = [start(hb_hbm.at[k], hb_ref.at[k - 1]) for k in (1, 2)]
    tables = [start(src_hbm, srcv_ref), start(send_hbm, sendv_ref)]
    vectors.wait()
    for t in range(RB // 2):
        tile = v_ref[:, 128 * t : 128 * (t + 1)].astype(f32)
        dup_ref[2 * t], dup_ref[2 * t + 1] = duplicate(tile, low)
    send.wait()
    emit_picks(msg_ref, dup_ref, lambda c: send_ref[0, c], low)
    picks_out = start(msg_ref.at[:, 0:MC, :], msg_hbm.at[:, 0:MC, :])
    src.wait()
    invert_slots(inv_ref, src_ref)
    weights_out = []
    for k in (1, 2):
        blocks[k - 1].wait()
        unpack_rows(rows_ref.at[k - 1], hb_ref.at[k - 1])
        for i in range(RB):
            block = unpacked_row(rows_ref.at[k - 1], i)
            pair = pair_ref.at[k - 1, i]
            store_pair(pair, block, block, low)
            wd_ref[i, :, 128 * (k - 1) : 128 * k] = pair[...].astype(bf16)
        half = slice(128 * (k - 1), 128 * k)
        weights_out.append(start(wd_ref.at[:, :, half], wd_hbm.at[0:RB, :, half]))
    keep_out = start(v_ref, keep_hbm.at[0:MC, :])
    for copy in tables:
        copy.wait()
    table_ref[...] = jnp.zeros(table_ref.shape, jnp.int32)
    table_ref[0:K, 0:RB] = srcv_ref[...]
    table_ref[K : K + 1, 0 : 2 * PEERS] = sendv_ref[...]
    table_out = start(table_ref, table_hbm.at[0:16, :])
    mirror_products(dup_ref, wd_ref, prod_ref)
    emit_mirror(msg_ref, prod_ref, inv_ref, low)
    mirror_out = start(msg_ref.at[:, MC : 2 * MC, :], msg_hbm.at[:, MC : 2 * MC, :])
    for copy in (keep_out, table_out, picks_out, *weights_out, mirror_out):
        copy.wait()


def local_sums(src_ref, v_ref, um_ref, um_ready, y_ref, dup_ref, dupb_ref, lhs_ref, mir_ref, *acc_refs):
    low = low_half()
    for t in range(RB // 2):
        tile = v_ref[:, 128 * t : 128 * (t + 1)].astype(f32)
        one, two = duplicate(tile, low)
        dup_ref[2 * t], dup_ref[2 * t + 1] = one, two
        dupb_ref[2 * t], dupb_ref[2 * t + 1] = one.astype(bf16), two.astype(bf16)

    def gather(i, _):
        for t, (k0, k1) in enumerate(LOCAL):
            j0 = i if k0 == 0 else jnp.minimum(src_ref[k0, i], RB - 1)
            j1 = jnp.minimum(src_ref[k1, i], RB - 1)
            lhs_ref[i, :, 128 * t : 128 * (t + 1)] = jnp.where(low, dup_ref[j0], dup_ref[j1]).astype(bf16)
        return 0

    lax.fori_loop(0, RB, gather, 0, unroll=8)
    um_ready()
    for i in range(RB):
        mir_ref[i] = dot(dupb_ref[i][:, 0:B], um_ref[i], NN)
    for i in range(RB):
        acc_refs[0][i, :, 0:B] = dot(lhs_ref[i], um_ref[i], NT)
    for acc_ref in acc_refs[1:]:
        acc_ref[...] = jnp.zeros(acc_ref.shape, f32)

    def scatter(i, _):
        for t, (k0, k1) in enumerate(LOCAL):
            j0 = i if k0 == 0 else jnp.minimum(src_ref[k0, i], RB - 1)
            j1 = jnp.minimum(src_ref[k1, i], RB - 1)
            part = mir_ref[i, :, 128 * t : 128 * (t + 1)]
            acc_refs[2 * (t % 2)][j0] += part
            acc_refs[2 * (t % 2) + 1][j1] += part
        return 0

    lax.fori_loop(0, RB, scatter, 0, unroll=8)
    for t in range(RB // 2):
        y_ref[:, 128 * t : 128 * (t + 1)] = folded(acc_refs[0], acc_refs[1], t, low) + folded(acc_refs[2], acc_refs[3], t, low)


def first_local_kernel(src_hbm, counts_hbm, v_hbm, hb_hbm, um_hbm, y_hbm, src_ref, counts_ref, v_ref, hb_ref, um_ref, y_ref, rows_ref, pair_ref, dup_ref, dupb_ref, lhs_ref, mir_ref, acc0_ref, acc1_ref, acc2_ref, acc3_ref, sems, hb_sems):
    low = low_half()
    start = starter(sems)
    counts = start(counts_hbm, counts_ref)

    def block_copies(t):
        k0, k1 = jnp.where(t == 0, 0, 2 * t + 2), 2 * t + 3
        return (
            pltpu.make_async_copy(hb_hbm.at[k0], hb_ref.at[2 * t], hb_sems.at[2 * t]),
            pltpu.make_async_copy(hb_hbm.at[k1], hb_ref.at[2 * t + 1], hb_sems.at[2 * t + 1]),
        )

    for t in range(len(LOCAL)):
        for copy in block_copies(t):
            copy.start()
    src = start(src_hbm, src_ref)
    vectors = start(v_hbm, v_ref)
    counts.wait()

    def relayout(t, _):
        for copy in block_copies(t):
            copy.wait()
        unpack_rows(rows_ref.at[0], hb_ref.at[2 * t])
        unpack_rows(rows_ref.at[1], hb_ref.at[2 * t + 1])
        k0, k1 = jnp.where(t == 0, 0, 2 * t + 2), 2 * t + 3
        lanes = pl.ds(pl.multiple_of(t * 128, 128), 128)
        for i in range(RB):
            count = counts_ref[i]
            one = jnp.where(k0 < count, unpacked_row(rows_ref.at[0], i), 0.0)
            two = jnp.where(k1 < count, unpacked_row(rows_ref.at[1], i), 0.0)
            store_pair(pair_ref.at[i], one, two, low)
            um_ref[i, :, lanes] = pair_ref[i].astype(bf16)
        return 0

    lax.fori_loop(0, len(LOCAL), relayout, 0)
    um_out = start(um_ref, um_hbm)
    src.wait()
    vectors.wait()
    local_sums(src_ref, v_ref, um_ref, lambda: None, y_ref, dup_ref, dupb_ref, lhs_ref, mir_ref, acc0_ref, acc1_ref, acc2_ref, acc3_ref)
    y_out = start(y_ref, y_hbm.at[0:MC, :])
    um_out.wait()
    y_out.wait()


def local_kernel(src_hbm, v_hbm, um_hbm, y_hbm, src_ref, v_ref, um_ref, y_ref, dup_ref, dupb_ref, lhs_ref, mir_ref, acc0_ref, acc1_ref, acc2_ref, acc3_ref, sems):
    start = starter(sems)
    vectors = start(v_hbm.at[0:MC, :], v_ref)
    src = start(src_hbm, src_ref)
    um = start(um_hbm, um_ref)
    vectors.wait()
    src.wait()
    local_sums(src_ref, v_ref, um_ref, um.wait, y_ref, dup_ref, dupb_ref, lhs_ref, mir_ref, acc0_ref, acc1_ref, acc2_ref, acc3_ref)
    start(y_ref, y_hbm.at[0:MC, :]).wait()


def remote_sum(table_ref, recv_ref, wd_ref, wd_ready, lhs_ref, low_ref, high_ref):
    lane = lax.broadcasted_iota(jnp.int32, (MC, 128), 1) // B

    def gather(i, _):
        for k in (1, 2):
            s = table_ref[k, i] - RB
            tile = recv_ref[s // 2, 0:MC, :].astype(f32)
            lhs_ref[i, :, 128 * (k - 1) : 128 * k] = jnp.where(lane == s % 2, tile, 0.0).astype(bf16)
        return 0

    lax.fori_loop(0, RB, gather, 0, unroll=8)
    wd_ready()
    for i in range(RB):
        low_ref[i, :, 0:B] = dot(lhs_ref[i], wd_ref[i], NT)
    high_ref[...] = jnp.zeros(high_ref.shape, f32)

    def scatter(q, _):
        tile = recv_ref[q, MC : 2 * MC, :].astype(f32)
        low_ref[table_ref[K, 2 * q]] += tile
        high_ref[table_ref[K, 2 * q + 1]] += tile
        return 0

    lax.fori_loop(0, PEERS, scatter, 0, unroll=8)


def folded(low_ref, high_ref, t, low):
    one, two = 2 * t, 2 * t + 1
    return jnp.where(
        low, low_ref[one] + pltpu.roll(high_ref[one], B, 1), pltpu.roll(low_ref[two], B, 1) + high_ref[two]
    )


def step_kernel(second, table_hbm, recv_ref, y_hbm, v_hbm, prev_hbm, wd_hbm, out_hbm, msg_hbm, table_ref, y_ref, v_ref, prev_ref, wd_ref, out_ref, msg_ref, lhs_ref, low_ref, high_ref, dup_ref, prod_ref, inv_ref, sems):
    low = low_half()
    start = starter(sems)
    table = start(table_hbm.at[0:16, :], table_ref)
    wd = start(wd_hbm.at[0:RB], wd_ref)
    terms = [start(y_hbm.at[0:MC, :], y_ref), start(v_hbm.at[0:MC, :], v_ref)]
    if second:
        terms.append(start(prev_hbm.at[0:MC, :], prev_ref))
    table.wait()
    invert_slots(inv_ref, table_ref)
    remote_sum(table_ref, recv_ref, wd_ref, wd.wait, lhs_ref, low_ref, high_ref)
    for copy in terms:
        copy.wait()
    for t in range(RB // 2):
        lanes = slice(128 * t, 128 * (t + 1))
        image = folded(low_ref, high_ref, t, low) + y_ref[:, lanes]
        if second:
            tile = 2.0 * (image - center_value * prev_ref[:, lanes].astype(f32)) / half_width - v_ref[:, lanes].astype(f32)
        else:
            tile = (image - center_value * v_ref[:, lanes].astype(f32)) / half_width
        tile = tile.astype(bf16)
        out_ref[:, lanes] = tile
        dup_ref[2 * t], dup_ref[2 * t + 1] = duplicate(tile.astype(f32), low)
    result_out = start(out_ref, out_hbm.at[0:MC, :])
    emit_picks(msg_ref, dup_ref, lambda c: table_ref[K, c], low)
    picks_out = start(msg_ref.at[:, 0:MC, :], msg_hbm.at[:, 0:MC, :])
    mirror_products(dup_ref, wd_ref, prod_ref)
    emit_mirror(msg_ref, prod_ref, inv_ref, low)
    mirror_out = start(msg_ref.at[:, MC : 2 * MC, :], msg_hbm.at[:, MC : 2 * MC, :])
    result_out.wait()
    picks_out.wait()
    mirror_out.wait()


def image_kernel(table_hbm, recv_ref, y_hbm, wd_hbm, *refs):
    own, other = refs[0:NY], refs[NY : 2 * NY]
    out_ref, table_ref, y_ref, wd_ref, lhs_ref, low_ref, high_ref, stack_ref, all_ref, sems = refs[2 * NY :]
    low = low_half()
    start = starter(sems)
    table = start(table_hbm.at[0:16, :], table_ref)
    wd = start(wd_hbm.at[0:RB], wd_ref)
    y_sum = start(y_hbm.at[0:MC, :], y_ref)
    y, c = lax.axis_index("y"), lax.axis_index("c")
    moves = [start(own[0], stack_ref.at[0:MC, :])]
    for d in range(NY):
        from_y = lax.rem(y + NY - SHIFTS[d], NY) * NC
        for block, core in ((own[d], c), (other[d], 1 - c)):
            moves.append(start(block, all_ref.at[pl.ds(pl.multiple_of((from_y + core) * MC, MC), MC), :]))
    table.wait()
    remote_sum(table_ref, recv_ref, wd_ref, wd.wait, lhs_ref, low_ref, high_ref)
    y_sum.wait()
    for t in range(RB // 2):
        lanes = slice(128 * t, 128 * (t + 1))
        stack_ref[MC : 2 * MC, lanes] = (folded(low_ref, high_ref, t, low) + y_ref[:, lanes]).astype(bf16)
    for copy in moves:
        copy.wait()
    part = dot(stack_ref[...], all_ref[...], NT).astype(bf16)
    for x in range(NX):
        out_ref[x] = part


def sum_x_kernel(in_ref, out_ref):
    total = in_ref[0].astype(f32)
    for x in range(1, NX):
        total = total + in_ref[x].astype(f32)
    total = total.astype(bf16)
    for z in range(NZ):
        out_ref[z] = total


def sum_z_kernel(in_ref, gram_ref, proj_ref):
    total = in_ref[0].astype(f32)
    for z in range(1, NZ):
        total = total + in_ref[z].astype(f32)
    gram_ref[...] = total[0:MC, :]
    proj_ref[...] = total[MC : 2 * MC, :]


VM = pl.BlockSpec(memory_space=pltpu.VMEM)
ANY = pl.BlockSpec(memory_space=pl.ANY)
HBM = pl.BlockSpec(memory_space=pltpu.HBM)
shape = jax.ShapeDtypeStruct


def limit(mib):
    return pltpu.CompilerParams(vmem_limit_bytes=int(mib * MIB))


LOCAL_COST = pl.CostEstimate(flops=2 * 2 * RB * 10 * MC * B * B, bytes_accessed=20 * MIB, transcendentals=0)


def semaphores(count):
    return pltpu.SemaphoreType.DMA((count,))


def on_device(vectors, hblocks, counts, sources, send_rows):
    cols, width = vectors.shape
    row_axes, rows = ("z", "x"), hblocks.shape[0]
    msg_shape = shape((PEERS, 2 * MC, 128), bf16)
    um_shape = shape((rows, B, LW), bf16)
    vec = pltpu.VMEM((cols, width), bf16)
    vec_sum = pltpu.VMEM((cols, width), f32)
    msg = pltpu.VMEM(msg_shape.shape, bf16)
    wd_scratch = pltpu.VMEM((rows, B, 256), bf16)
    um_scratch = pltpu.VMEM(um_shape.shape, bf16)
    dup = pltpu.VMEM((rows, MC, 128), f32)
    dupb = pltpu.VMEM((rows, MC, 128), bf16)
    acc = pltpu.VMEM((rows, MC, 128), f32)
    prod = pltpu.VMEM((2 * rows, MC, 128), f32)
    inv = pltpu.SMEM((2 * PEERS,), jnp.int32)
    src = pltpu.SMEM((K, rows), jnp.int32)
    table_scratch = pltpu.SMEM((16, 128), jnp.int32)
    lhs = pltpu.VMEM((rows, MC, LW), bf16)
    lhs_remote = pltpu.VMEM((rows, MC, 256), bf16)
    mir = pltpu.VMEM((rows, MC, LW), f32)
    unpacked = pltpu.VMEM((2, STRIDE * 32, 128), f32)

    blocks = hblocks.transpose(1, 0, 2)
    sources = sources.T
    message, wd, table, kept = pl.pallas_call(
        first_message_kernel,
        out_shape=(
            msg_shape,
            shape((4 * rows, B, 256), bf16),
            shape((TABLE, 128), jnp.int32),
            shape((ROOM, width), bf16),
        ),
        in_specs=[HBM] * 4,
        out_specs=(HBM,) * 4,
        scratch_shapes=[
            src,
            pltpu.SMEM((1, 2 * PEERS), jnp.int32),
            pltpu.VMEM((K, rows), jnp.int32),
            pltpu.VMEM((1, 2 * PEERS), jnp.int32),
            pltpu.VMEM((16, 128), jnp.int32),
            vec,
            pltpu.VMEM((2, rows, B * B), bf16),
            msg,
            wd_scratch,
            unpacked,
            pltpu.VMEM((2, rows, B, 128), f32),
            dup,
            prod,
            inv,
            semaphores(13),
        ],
        compiler_params=limit(60),
        name="first_message",
    )(sources, send_rows[None], vectors, blocks)

    def exchange(message):
        return lax.all_to_all(message, row_axes, split_axis=0, concat_axis=0, tiled=True)

    received = exchange(message)
    local_scratch = [dup, dupb, lhs, mir, acc, acc, acc, acc]
    um, local = pl.pallas_call(
        first_local_kernel,
        out_shape=(um_shape, shape((ROOM, width), f32)),
        in_specs=[HBM] * 4,
        out_specs=(HBM, HBM),
        scratch_shapes=[
            src,
            pltpu.SMEM((rows,), jnp.int32),
            vec,
            pltpu.VMEM((2 * len(LOCAL), rows, B * B), bf16),
            um_scratch,
            vec_sum,
            unpacked,
            pltpu.VMEM((rows, B, 128), f32),
        ]
        + local_scratch
        + [semaphores(5), semaphores(2 * len(LOCAL))],
        compiler_params=limit(60),
        name="first_local",
    )(sources, counts, vectors, blocks)

    def local_part(block):
        return pl.pallas_call(
            local_kernel,
            out_shape=shape((ROOM, width), f32),
            in_specs=[HBM] * 3,
            out_specs=HBM,
            scratch_shapes=[src, vec, um_scratch, vec_sum] + local_scratch + [semaphores(4)],
            compiler_params=limit(60),
            cost_estimate=LOCAL_COST,
            name="local_product",
        )(sources, block, um)

    def next_step(second, received, local, previous):
        return pl.pallas_call(
            lambda *refs: step_kernel(second, *refs),
            out_shape=(shape((cols if second else ROOM, width), bf16), msg_shape),
            in_specs=[HBM, VM] + [HBM] * 4,
            out_specs=(HBM, HBM),
            scratch_shapes=[table_scratch, vec_sum, vec, vec, wd_scratch, vec, msg, lhs_remote, acc, acc, dup, prod, inv]
            + [semaphores(9)],
            compiler_params=limit(51.6),
            name="second_step" if second else "first_step",
        )(table, received, local, kept, previous, wd)

    first, message = next_step(False, received, local, kept)
    received = exchange(message)
    local = local_part(first)
    filtered, message = next_step(True, received, local, first)
    received = exchange(message)
    local = local_part(filtered)
    own = [filtered] + [
        lax.ppermute(filtered, "y", [(y, (y + d) % NY) for y in range(NY)]) for d in SHIFTS[1:]
    ]
    local, *passed = lax.optimization_barrier((local, *own[1:]))
    own = own[:1] + passed
    other = [lax.ppermute(block, "c", [(0, 1), (1, 0)]) for block in own]
    part = pl.pallas_call(
        image_kernel,
        out_shape=shape((NX, 2 * MC, NY * NC * MC), bf16),
        in_specs=[HBM, VM, HBM, HBM, HBM] + [ANY] * (2 * NY - 1),
        out_specs=VM,
        scratch_shapes=[
            table_scratch,
            vec_sum,
            wd_scratch,
            lhs_remote,
            acc,
            acc,
            pltpu.VMEM((2 * MC, width), bf16),
            pltpu.VMEM((NY * NC * MC, width), bf16),
            semaphores(5 + 2 * NY),
        ],
        compiler_params=limit(51.6),
        name="image",
    )(table, received, local, wd, *own, *other)
    part = lax.all_to_all(part, "x", split_axis=0, concat_axis=0, tiled=True)
    part = pl.pallas_call(
        sum_x_kernel,
        out_shape=shape((NZ,) + part.shape[1:], bf16),
        compiler_params=limit(4),
        name="sum_x",
    )(part)
    part = lax.all_to_all(part, "z", split_axis=0, concat_axis=0, tiled=True)
    gram, projected = pl.pallas_call(
        sum_z_kernel,
        out_shape=(shape((MC, NY * NC * MC), f32),) * 2,
        compiler_params=limit(4),
        name="sum_z",
    )(part)
    return filtered, gram.T, projected.T


def solution(mesh):
    axes = Mesh(mesh.devices.reshape(NZ, NX, NY, NC), ("z", "x", "y", "c"))
    row, col = ("z", "x"), ("y", "c")
    return jax.shard_map(
        on_device,
        mesh=axes,
        in_specs=(P(col, row), P(row, None, None), P(row), P(row, None), P(row)),
        out_specs=(P(col, row), P(None, col), P(None, col)),
        check_vma=False,
    )
```
